32 devices in a mesh: groups: 2 (over x), seq: 8 (over z, y), exp: 2 (over core).
Axes of the slice: x: 2, y: 2, z: 4, core: 2. Of those that a mesh axis runs over, the one named last changes fastest.
Arguments:
- stream: bfloat16 [2048, 2048], P(('groups', 'seq', 'exp')), parts along dimension 0, may hold values from -5 to 5
- queries: bfloat16 [2048, 4096], P(('groups', 'seq'), 'exp'), parts along dimension 0, may hold values from -131 to 131
- key_rows: bfloat16 [2048, 512], P(('groups', 'seq'), 'exp'), parts along dimension 0, may hold values from -4 to 4
- value_rows: bfloat16 [2048, 512], P(('groups', 'seq'), 'exp'), parts along dimension 0, may hold values from -4 to 4
- out_weight: bfloat16 [2048, 4096], P('seq', 'exp'), may hold values from -0.375 to 0.375
- norm_gain: float32 [2048], replicated, may hold values from 0.1 to 1.9
- expert_ids: int32 [2048, 8], P(('groups', 'seq', 'exp')), parts along dimension 0, may hold values from 0 to 63, all different within a row; in each aligned block of 64 rows (0 to 63, 64 to 127, ...) at most 12 rows name the same one
- gate_weights: float32 [2048, 8], P(('groups', 'seq', 'exp')), parts along dimension 0, may hold values from 0.05 to 0.5
- expert_in: bfloat16 [64, 2048, 1536], P(('seq', 'exp')), may hold values from -0.125 to 0.125
- expert_out: bfloat16 [64, 768, 2048], P(('seq', 'exp')), may hold values from -0.21875 to 0.21875
Outputs:
- layer_out: bfloat16 [2048, 2048], P(('groups', 'seq', 'exp')), parts along dimension 0
The draws below stay inside these ranges and needn't reach their ends.
There are 2 independent parts, one for each index of `groups`. The reference program is written for one: setup_inputs(seed, part) draws one part's arguments, and reference() takes and returns one part's arrays. A program takes and returns all parts, laid end to end along the dimension named above; an argument that names none is the same for every part. Nothing has to cross between parts.
Inputs may be any that keep to these rules, and one draw needn't show every extreme that they name: `expert_ids`: each row names 8 different experts. Among the 64 rows of one device (aligned blocks of rows), no expert is named more than 12 times, a bound that some block reaches.
All inputs are finite; a program needn't handle non-finite values.
Results may differ from the reference program's by a relative error of at most 0.0095.
Values may be sent and summed in bfloat16 or wider, within the bound.
No kernel may reach another device: no remote copies, remote signals or barrier semaphores. Data moves between devices by JAX's collectives and lax.ppermute only.
A program may use at most 128 MiB of HBM per device.

```python
import math
import jax
import jax.numpy as jnp
import numpy as np
from jax import lax

D = 2048
H = 32
KVH = 4
HD = 128
F = 768
EXPERTS = 64
TOPK = 8
CAP = 12
SPAN = 128
SEQLEN = 1024
MROWS = 64


def draw_pair(key):
    base = jax.random.fold_in(key, 7101)
    key_part, query_part = jax.random.split(base, 2)
    per_group = H // KVH
    keyed = jnp.clip(jax.random.normal(key_part, (SEQLEN, KVH, HD), jnp.float32), -3.5, 3.5)
    queried = jnp.clip(jax.random.normal(query_part, (SEQLEN, KVH, per_group, HD), jnp.float32), -3.5, 3.5)
    return (queried, keyed)


def draw_queries(key, part):
    queried, keyed = draw_pair(key)
    return queried.reshape(SEQLEN, H * HD).astype(jnp.bfloat16)


def draw_key_rows(key, part):
    queried, keyed = draw_pair(key)
    return keyed.reshape(SEQLEN, KVH * HD).astype(jnp.bfloat16)


def steps_of(key, shape, shards, least, high):
    def one(axis_at, parts):
        heights = jax.random.uniform(jax.random.fold_in(jax.random.fold_in(key, 6), axis_at), (parts,), jnp.float32, least / len(shards), high / len(shards))
        return jnp.repeat(jnp.exp(heights), shape[axis_at] // parts).reshape((-1,) + (1,) * (len(shape) - axis_at - 1))

    loudness = one(*shards[0])
    for cut in shards[1:]:
        loudness = loudness * one(*cut)
    return loudness


def assign_block(stream_key, own, number, rows, count, top, most, slope):
    sequence = jax.random.permutation(stream_key, count)
    packed, common = shares(count, rows * top, most, slope, True), shares(count, rows * top, most, slope, False)
    places = jnp.arange(count)

    def named(tallies, rotation):
        used = int((tallies > 0).sum())
        fixed = max(1, used // 4)
        passed = fixed + (places - fixed + rotation * (used - fixed)) % max(1, count - fixed)
        return jnp.zeros((count,), jnp.int32).at[sequence[jnp.where(places < fixed, places, passed)]].set(jnp.asarray(tallies, jnp.int32))

    tallies = jnp.where(number % 4 == 0, named(packed, number // 4), named(common, number - number // 4 - 1))
    mixed = jax.random.permutation(jax.random.fold_in(own, 3), count)
    giver, receiver = mixed[0:count // 2 * 2:2], mixed[1:count // 2 * 2:2]
    margin = jnp.minimum(tallies[giver] - 1, most - tallies[receiver]) // 2
    margin = jnp.where((giver == sequence[0]) | (receiver == sequence[0]) | (tallies[receiver] == 0), 0, jnp.maximum(margin, 0))
    passed = jax.random.randint(jax.random.fold_in(own, 4), (count // 2,), 0, 1 << 20) % (margin + 1)
    tallies = tallies.at[giver].add(-passed).at[receiver].add(passed)
    members = jnp.searchsorted(jnp.cumsum(tallies), jnp.arange(rows * top), side="right").astype(jnp.int32)
    listing = members.reshape(top, rows).T
    listing = listing[jax.random.permutation(jax.random.fold_in(own, 1), rows)]
    rotation = jax.random.randint(jax.random.fold_in(own, 2), (rows, 1), 0, top)
    return jnp.take_along_axis(listing, (jnp.arange(top)[None, :] + rotation) % top, axis=1)


def shares(count, total, most, lean, full):
    loads = [(1 << 20) // math.isqrt(grade ** lean) + 1 for grade in range(1, count + 1)]
    largest = most if full else min(most, max(-(-total // count), total * loads[0] // sum(loads)))
    least = 1 if total - largest >= count - 1 else 0
    holding, rest = [largest] + [least] * (count - 1), total - largest - least * (count - 1)
    while rest > 0:
        movable = [i for i in range(1, count) if holding[i] < largest] or [i for i in range(1, count) if holding[i] < most]
        pool, remaining = sum([loads[i] for i in movable]), rest
        for i in movable:
            more = min(most - holding[i], max(1, remaining * loads[i] // pool), rest)
            holding[i] = holding[i] + more
            rest = rest - more
    return np.array(holding)


def normal_values(rng, shape, deviation, most, pieces=(), held_as=jnp.bfloat16):
    result = deviation * jax.random.normal(rng, shape, jnp.float32)
    if pieces:
        result = result * steps_of(rng, shape, pieces, -0.22, 0.18)
    return jnp.clip(result, -most, most).astype(held_as)


def setup_inputs(seed: int = 0, part: int = 0) -> dict:
    key_list = jax.random.split(jax.random.key(seed), 11)
    own_keys = jax.random.split(jax.random.fold_in(key_list[10], part), 11)
    stream = normal_values(own_keys[0], (SEQLEN, D), 1.0, 5.0, ((0, 16),))
    queries = draw_queries(jax.random.fold_in(jax.random.fold_in(key_list[10], part), 71), part)
    key_rows = draw_key_rows(jax.random.fold_in(jax.random.fold_in(key_list[10], part), 71), part)
    value_rows = normal_values(own_keys[3], (SEQLEN, KVH * HD), 1.0, 4.0, ((0, 8), (1, 2)))
    out_weight = normal_values(key_list[4], (D, H * HD), (H * HD // 16) ** -0.5, 0.375, ((0, 8), (1, 2)))
    norm_gain = jnp.clip(1.0 + 0.18 * jax.random.normal(key_list[5], (D,), jnp.float32), 0.1, 1.9)
    expert_ids_keys = jax.random.split(jax.random.fold_in(own_keys[6], 1), SEQLEN // MROWS)
    expert_ids_turns = jax.random.permutation(jax.random.fold_in(own_keys[6], 3), SEQLEN // MROWS)
    expert_ids = jax.vmap(lambda own, number: assign_block(jax.random.fold_in(own_keys[6], 2), own, number, MROWS, EXPERTS, TOPK, CAP, 2))(expert_ids_keys, expert_ids_turns).reshape((SEQLEN, TOPK))
    gate_weights = jnp.clip(jnp.exp(math.log(0.5) - 2.3025851 * jax.random.uniform(own_keys[7], (SEQLEN, TOPK), jnp.float32) ** steps_of(own_keys[7], (SEQLEN, TOPK), ((0, 16),), -0.2, 0.2)), 0.05, 0.5)
    expert_in = normal_values(key_list[8], (EXPERTS, D, 2 * F), D ** -0.5, 0.125, ((0, 16),))
    expert_out = normal_values(key_list[9], (EXPERTS, F, D), F ** -0.5, 0.21875, ((0, 16),))
    return {"stream": stream, "queries": queries, "key_rows": key_rows, "value_rows": value_rows, "out_weight": out_weight, "norm_gain": norm_gain, "expert_ids": expert_ids, "gate_weights": gate_weights, "expert_in": expert_in, "expert_out": expert_out}


def attend_block(query_block, block_start, key_rows, value_rows):
    rows = query_block.shape[0]
    per_group = H // KVH
    grouped = query_block.reshape(rows, KVH, per_group, HD).astype(jnp.float32)
    keyed = key_rows.reshape(-1, KVH, HD).astype(jnp.float32)
    valued = value_rows.reshape(-1, KVH, HD).astype(jnp.float32)
    scores = jnp.einsum('tghd,sgd->gths', grouped, keyed) / jnp.sqrt(jnp.float32(HD))
    query_pos = block_start + jnp.arange(rows, dtype=jnp.int32)
    key_pos = jnp.arange(keyed.shape[0], dtype=jnp.int32)
    allowed = (key_pos[None, :] <= query_pos[:, None])[None, :, None, :]
    scores = jnp.where(allowed, scores, jnp.float32(-1e+30))
    largest = lax.optimization_barrier(jnp.max(scores, axis=-1, keepdims=True))
    exps = jnp.where(allowed, jnp.exp(scores - largest), jnp.float32(0.0))
    total = lax.optimization_barrier(jnp.sum(exps, axis=-1))
    probs = exps.astype(jnp.bfloat16)
    summed = jnp.einsum('gths,sgd->gthd', probs.astype(jnp.float32), valued)
    context = summed / total[..., None]
    return context.transpose(1, 0, 2, 3).reshape(rows, H * HD).astype(jnp.bfloat16)

def reference(stream, queries, key_rows, value_rows, out_weight, norm_gain, expert_ids, gate_weights, expert_in, expert_out):
    block_count = SEQLEN // SPAN
    blocks = queries.reshape(block_count, SPAN, H * HD)
    starts = jnp.arange(block_count, dtype=jnp.int32) * SPAN
    context = lax.map(lambda pair: attend_block(pair[0], pair[1], key_rows, value_rows), (blocks, starts))
    context = context.reshape(SEQLEN, H * HD)
    attn_out = jnp.dot(context, out_weight.T, preferred_element_type=jnp.float32)
    mixed = stream.astype(jnp.float32) + attn_out
    normed = (mixed * lax.rsqrt(lax.optimization_barrier(jnp.mean(mixed * mixed, axis=-1, keepdims=True)) + 1e-06) * norm_gain).astype(jnp.bfloat16)
    group_count = SEQLEN // MROWS
    assigned = MROWS * TOPK
    flat_ids = expert_ids.reshape(group_count, assigned)
    onehot = (flat_ids[..., None] == jnp.arange(EXPERTS, dtype=jnp.int32)[None, None, :]).astype(jnp.int32)
    earlier = jnp.cumsum(onehot, axis=1) - onehot
    slots = lax.optimization_barrier(jnp.sum(earlier * onehot, axis=-1)).astype(jnp.int32)
    group_index = jnp.arange(group_count, dtype=jnp.int32)[:, None]
    token_index = group_index * MROWS + jnp.arange(assigned, dtype=jnp.int32)[None, :] // TOPK
    position = (flat_ids * (group_count * CAP) + group_index * CAP + slots).astype(jnp.int32).reshape(-1)
    table = jnp.zeros((EXPERTS * group_count * CAP,), jnp.int32).at[position].set(token_index.reshape(-1).astype(jnp.int32))

    def run_expert(pack):
        rows_index, first, second = pack
        inputs = normed[rows_index]
        gate_up = jnp.dot(inputs, first, preferred_element_type=jnp.float32)
        act = (jax.nn.silu(gate_up[:, :F]) * gate_up[:, F:]).astype(jnp.bfloat16)
        return jnp.dot(act, second, preferred_element_type=jnp.float32).astype(jnp.bfloat16)
    results = lax.map(run_expert, (table.reshape(EXPERTS, group_count * CAP), expert_in, expert_out))
    picked = results.reshape(-1, D)[position].reshape(SEQLEN, TOPK, D)
    combined = lax.optimization_barrier(jnp.sum(gate_weights[..., None] * picked.astype(jnp.float32), axis=1))
    return (mixed + combined).astype(jnp.bfloat16)
```

```python
import jax
import jax.numpy as jnp
from jax import lax
from jax.experimental import pallas as pl
from jax.experimental.pallas import tpu as pltpu
from jax.sharding import PartitionSpec as P

HD = 128
CAP = 12
FCHUNK = 256


def ring(size, step):
    return [(i, (i + 2 * step) % size) for i in range(size)]


def swap(size):
    return [(i, i ^ 1) for i in range(size)]


def gather_meta(meta, size, depth):
    along = jnp.stack([meta] + [lax.ppermute(meta, "seq", ring(size, d)) for d in range(1, depth)])
    both = jnp.stack([along, lax.ppermute(along, "seq", swap(size))], axis=1)
    return jnp.stack([both, lax.ppermute(both, "exp", swap(2))], axis=2)


def routing(ids, gates, first, local_experts):
    blocks, rows, _ = ids.shape
    subs = blocks // 4
    experts = first + jnp.arange(local_experts, dtype=jnp.int32)
    match = ids[..., None] == experts
    hit = jnp.any(match, axis=2)
    weight = jnp.sum(jnp.where(match, gates[..., None], 0.0), axis=2)
    count = hit.astype(jnp.int32)
    place = jnp.where(hit, jnp.cumsum(count, axis=1) - count, -1)
    place = place.reshape(subs, 4, rows, local_experts).transpose(3, 0, 1, 2)
    weight = weight.reshape(subs, 4, rows, local_experts).transpose(3, 0, 1, 2)
    chosen = place[:, :, :, None, :] == jnp.arange(CAP, dtype=jnp.int32)[:, None]
    row_gate = jnp.sum(jnp.where(chosen, weight[:, :, :, None, :], 0.0), axis=-1)
    row_gate = row_gate.reshape(local_experts, subs * 4 * CAP, 1)
    diagonal = jnp.eye(4, dtype=bool)[:, None, :, None]
    full = chosen[:, :, :, :, None, :] & diagonal
    select = full.reshape(local_experts, subs, 4 * CAP, 4 * rows).astype(jnp.bfloat16)
    spread = select.transpose(1, 3, 0, 2).reshape(subs, 4 * rows, local_experts * 4 * CAP)
    return select, spread, row_gate


def expert_kernel(x_ref, select_ref, spread_ref, gate_ref, wg_ref, wu_ref, wo_ref, out_ref, xg, acc, res):
    expert, chunk = pl.program_id(0), pl.program_id(1)
    last = pl.num_programs(1) - 1
    subs, slots = select_ref.shape[1], select_ref.shape[2]
    tokens = x_ref.shape[1]

    @pl.when(chunk == 0)
    def _():
        for s in range(subs):
            xg[s * slots : (s + 1) * slots, :] = jnp.dot(
                select_ref[expert, s], x_ref[s], preferred_element_type=jnp.float32
            ).astype(jnp.bfloat16)

    rows = xg[...]
    gate = jnp.dot(rows, wg_ref[0], preferred_element_type=jnp.float32)
    up = jnp.dot(rows, wu_ref[0], preferred_element_type=jnp.float32)
    act = (gate / (1.0 + jnp.exp(-gate)) * up).astype(jnp.bfloat16)
    part = jnp.dot(act, wo_ref[0], preferred_element_type=jnp.float32)

    @pl.when(chunk == 0)
    def _():
        acc[...] = part

    @pl.when(chunk > 0)
    def _():
        acc[...] += part

    @pl.when(chunk == last)
    def _():
        scaled = (acc[...] * gate_ref[expert]).astype(jnp.bfloat16)
        for s in range(subs):
            res[s, expert] = scaled[s * slots : (s + 1) * slots, :]

    @pl.when((chunk == last) & (expert == pl.num_programs(0) - 1))
    def _():
        for s in range(subs):
            out_ref[s * tokens : (s + 1) * tokens, :] = jnp.dot(
                spread_ref[s], res[s].reshape(-1, res.shape[-1]), preferred_element_type=jnp.float32
            ).astype(jnp.bfloat16)


def run_experts(x, select, spread, row_gate, expert_in, expert_out):
    subs, tokens, width = x.shape
    local_experts, hidden, _ = expert_out.shape
    slots = select.shape[2]
    chunks = hidden // FCHUNK
    flops = local_experts * subs * slots * width * hidden * 6
    moved = (expert_in.size + expert_out.size + 2 * x.size) * 2
    whole = lambda shape: pl.BlockSpec(shape, lambda e, f: (0,) * len(shape), pipeline_mode=pl.Buffered(1))
    return pl.pallas_call(
        expert_kernel,
        grid=(local_experts, chunks),
        out_shape=jax.ShapeDtypeStruct((subs * tokens, width), jnp.bfloat16),
        in_specs=[
            whole(x.shape),
            whole(select.shape),
            whole(spread.shape),
            whole(row_gate.shape),
            pl.BlockSpec((1, width, FCHUNK), lambda e, f: (e, 0, f)),
            pl.BlockSpec((1, width, FCHUNK), lambda e, f: (e, 0, f + chunks)),
            pl.BlockSpec((1, FCHUNK, width), lambda e, f: (e, f, 0)),
        ],
        out_specs=whole((subs * tokens, width)),
        scratch_shapes=[
            pltpu.VMEM((subs * slots, width), jnp.bfloat16),
            pltpu.VMEM((subs * slots, width), jnp.float32),
            pltpu.VMEM((subs, local_experts, slots, width), jnp.bfloat16),
        ],
        compiler_params=pltpu.CompilerParams(vmem_limit_bytes=48 * 1024 * 1024),
        cost_estimate=pl.CostEstimate(flops=flops, bytes_accessed=moved, transcendentals=0),
        name="experts",
    )(x, select, spread, row_gate, expert_in, expert_in, expert_out)


def wide(value):
    return value.astype(jnp.float32)


def expert_block(mixed, norm_gain, expert_ids, gate_weights, expert_in, expert_out):
    size = lax.axis_size("seq")
    depth = size // 2
    rows, width = mixed.shape
    local_experts = expert_in.shape[0]
    first = (lax.axis_index("seq") * 2 + lax.axis_index("exp")) * local_experts
    gate_high = gate_weights.astype(jnp.bfloat16)
    gate_low = (gate_weights - wide(gate_high)).astype(jnp.bfloat16)
    meta = jnp.concatenate([expert_ids.astype(jnp.bfloat16), gate_high, gate_low], axis=1)
    meta = gather_meta(meta, size, depth)
    top = expert_ids.shape[1]
    passes = [list(range(depth // 2)), list(range(depth // 2, depth))]
    routes = []
    for group in passes:
        own = meta[group[0] : group[-1] + 1].transpose(2, 0, 1, 3, 4).reshape(-1, rows, 3 * top)
        ids = own[..., :top].astype(jnp.int32)
        gates = wide(own[..., top : 2 * top]) + wide(own[..., 2 * top :])
        routes.append(routing(ids, gates, first, local_experts))

    normed = (
        mixed * lax.rsqrt(jnp.mean(mixed * mixed, axis=-1, keepdims=True) + 1e-06) * norm_gain
    ).astype(jnp.bfloat16)
    along, across = [normed], []
    for d in range(depth):
        if d + 1 < depth:
            along.append(lax.ppermute(along[d], "seq", ring(size, 1)))
        across.append(lax.ppermute(along[d], "seq", swap(size)))
    total = mixed
    for group, route in zip(passes, routes):
        mine = jnp.concatenate([part for d in group for part in (along[d], across[d])])
        other = lax.ppermute(mine, "exp", swap(2))
        x = jnp.concatenate([mine, other]).reshape(-1, 4 * rows, width)
        out = run_experts(x, *route, expert_in, expert_out).reshape(2, len(group), 2, rows, width)
        arrived = lax.ppermute(out[1], "exp", swap(2))
        pair = wide(out[0]) + wide(arrived)
        for place, d in enumerate(group):
            there = lax.ppermute(pair[place, 1].astype(jnp.bfloat16), "seq", swap(size))
            chip = pair[place, 0] + wide(there)
            if d:
                chip = wide(lax.ppermute(chip.astype(jnp.bfloat16), "seq", ring(size, -d)))
            total = total + chip
    return total.astype(jnp.bfloat16)


neg_large = -1e30


def attend_piece(state, query_group, key_piece, value_piece, key_start, query_start):
    largest, total, summed = state
    length = key_piece.shape[0]
    groups = query_group.shape[1]
    head_size = query_group.shape[3]
    rows = query_group.shape[0]
    keyed = key_piece.reshape(length, groups, head_size)
    valued = value_piece.reshape(length, groups, head_size)
    scores = jnp.einsum(
        "tghd,sgd->gths", query_group, keyed, preferred_element_type=jnp.float32
    ) / jnp.sqrt(jnp.float32(head_size))
    query_pos = query_start + jnp.arange(rows, dtype=jnp.int32)
    key_pos = key_start + jnp.arange(length, dtype=jnp.int32)
    allowed = (key_pos[None, :] <= query_pos[:, None])[None, :, None, :]
    scores = jnp.where(allowed, scores, neg_large)
    new_largest = jnp.maximum(largest, jnp.max(scores, axis=-1))
    rescale = jnp.exp(largest - new_largest)
    exps = jnp.where(allowed, jnp.exp(scores - new_largest[..., None]), 0.0)
    total = total * rescale + jnp.sum(exps, axis=-1)
    summed = summed * rescale[..., None] + jnp.einsum(
        "gths,sgd->gthd", exps.astype(jnp.bfloat16), valued, preferred_element_type=jnp.float32
    )
    return (new_largest, total, summed)


def on_device(
    stream,
    queries,
    key_rows,
    value_rows,
    out_weight,
    norm_gain,
    expert_ids,
    gate_weights,
    expert_in,
    expert_out,
):
    rows = queries.shape[0]
    local_groups = key_rows.shape[1] // HD
    per_group = queries.shape[1] // (local_groups * HD)
    query_group = queries.reshape(rows, local_groups, per_group, HD)
    query_start = lax.axis_index("seq") * rows
    initial = (
        jnp.full((local_groups, rows, per_group), neg_large, jnp.float32),
        jnp.zeros((local_groups, rows, per_group), jnp.float32),
        jnp.zeros((local_groups, rows, per_group, HD), jnp.float32),
    )
    state = initial
    key_piece = lax.all_gather(key_rows, "seq", axis=0, tiled=True)
    value_piece = lax.all_gather(value_rows, "seq", axis=0, tiled=True)
    length = key_piece.shape[0]
    count = length // 512
    key_blocks = key_piece.reshape(count, 512, key_piece.shape[1])
    value_blocks = value_piece.reshape(count, 512, value_piece.shape[1])
    offsets = jnp.arange(count, dtype=jnp.int32) * 512

    def step(carry, block):
        return (attend_piece(carry, query_group, block[0], block[1], block[2], query_start), None)

    state, unused = lax.scan(step, state, (key_blocks, value_blocks, offsets))
    largest, total, summed = state
    context = (
        (summed / total[..., None]).transpose(1, 0, 2, 3).reshape(rows, -1).astype(jnp.bfloat16)
    )
    seq_count = lax.axis_size("seq")
    exp_count = lax.axis_size("exp")
    local_rows = stream.shape[0]
    partial_heads = lax.dot_general(
        context,
        lax.all_gather(out_weight, "seq", axis=0, tiled=True),
        (((1,), (1,)), ((), ())),
        preferred_element_type=jnp.float32,
    )
    attn_out = lax.psum_scatter(
        partial_heads.astype(jnp.bfloat16), "exp", scatter_dimension=0, tiled=True
    ).astype(jnp.float32)
    mixed = stream.astype(jnp.float32) + attn_out
    return expert_block(mixed, norm_gain, expert_ids, gate_weights, expert_in, expert_out)


def solution(mesh):
    in_specs = (
        P(("groups", "seq", "exp"), None),
        P(("groups", "seq"), "exp"),
        P(("groups", "seq"), "exp"),
        P(("groups", "seq"), "exp"),
        P("seq", "exp"),
        P(),
        P(("groups", "seq", "exp"), None),
        P(("groups", "seq", "exp"), None),
        P(("seq", "exp"), None, None),
        P(("seq", "exp"), None, None),
    )
    out_specs = P(("groups", "seq", "exp"), None)
    return jax.shard_map(
        on_device, mesh=mesh, in_specs=in_specs, out_specs=out_specs, check_vma=False
    )
```

```python
import jax
import jax.numpy as jnp
from jax import lax
from jax.experimental import pallas as pl
from jax.experimental.pallas import tpu as pltpu
from jax.sharding import PartitionSpec as P

HD = 128
CAP = 12
FCHUNK = 768


def ring(size, step):
    return [(i, (i + 2 * step) % size) for i in range(size)]


def swap(size):
    return [(i, i ^ 1) for i in range(size)]


neg_large = -1e30


def wide(value):
    return value.astype(jnp.float32)


def attend_kernel(starts_ref, key_pos_ref, query_ref, keyed_ref, out_ref):
    rows = query_ref.shape[1]
    heads = query_ref.shape[2] // HD
    stacked = jnp.concatenate([query_ref[0, :, h * HD : (h + 1) * HD] for h in range(heads)], axis=0)
    scores = lax.dot_general(
        stacked, keyed_ref[:, :HD], (((1,), (1,)), ((), ())), preferred_element_type=jnp.float32
    )
    offset = lax.broadcasted_iota(jnp.int32, (heads * rows, 1), 0) % rows
    allowed = key_pos_ref[...] <= starts_ref[pl.program_id(0)] + offset
    scores = jnp.where(allowed, scores, neg_large)
    largest = jnp.max(scores, axis=-1, keepdims=True)
    exps = jnp.exp((scores - largest) * (HD**-0.5))
    total = jnp.sum(exps, axis=-1, keepdims=True)
    summed = jnp.dot(exps.astype(jnp.bfloat16), keyed_ref[:, HD:], preferred_element_type=jnp.float32)
    context = (summed / total).astype(jnp.bfloat16)
    for h in range(heads):
        out_ref[0, :, h * HD : (h + 1) * HD] = context[h * rows : (h + 1) * rows]


def attend(starts, key_pos, query_blocks, keyed):
    blocks, rows, columns = query_blocks.shape
    length = keyed.shape[0]
    work = blocks * rows * columns * length
    return pl.pallas_call(
        attend_kernel,
        grid_spec=pltpu.PrefetchScalarGridSpec(
            num_scalar_prefetch=1,
            grid=(blocks,),
            in_specs=[
                pl.BlockSpec((1, length), lambda i, s: (0, 0)),
                pl.BlockSpec((1, rows, columns), lambda i, s: (i, 0, 0)),
                pl.BlockSpec((length, 2 * HD), lambda i, s: (0, 0)),
            ],
            out_specs=pl.BlockSpec((1, rows, columns), lambda i, s: (i, 0, 0)),
        ),
        out_shape=jax.ShapeDtypeStruct(query_blocks.shape, jnp.bfloat16),
        compiler_params=pltpu.CompilerParams(vmem_limit_bytes=32 * 1024 * 1024),
        cost_estimate=pl.CostEstimate(flops=4 * work, bytes_accessed=4 * query_blocks.size, transcendentals=work // HD),
        name="attend",
    )(starts, key_pos, query_blocks, keyed)


def project_kernel(place_ref, own_ref, other_ref, own_weight_ref, other_weight_ref, out_ref):
    dims = (((1,), (1,)), ((), ()))
    out_ref[...] = (
        lax.dot_general(own_ref[...], own_weight_ref[0], dims, preferred_element_type=jnp.float32)
        + lax.dot_general(other_ref[...], other_weight_ref[0], dims, preferred_element_type=jnp.float32)
    ).astype(jnp.bfloat16)


def project(place, own, other, own_weight, other_weight):
    blocks, features, columns = own_weight.shape
    rows = own.shape[0]
    if features % HD:
        order = jnp.argsort(place)
        weight = jnp.concatenate([own_weight, other_weight], axis=2)[order]
        both = jnp.concatenate([own, other], axis=1)
        result = jnp.einsum("rc,bfc->rbf", both, weight, preferred_element_type=jnp.float32)
        return result.reshape(rows, -1).astype(jnp.bfloat16)
    return pl.pallas_call(
        project_kernel,
        grid_spec=pltpu.PrefetchScalarGridSpec(
            num_scalar_prefetch=1,
            grid=(blocks,),
            in_specs=[
                pl.BlockSpec((rows, columns), lambda i, p: (0, 0)),
                pl.BlockSpec((rows, columns), lambda i, p: (0, 0)),
                pl.BlockSpec((1, features, columns), lambda i, p: (i, 0, 0)),
                pl.BlockSpec((1, features, columns), lambda i, p: (i, 0, 0)),
            ],
            out_specs=pl.BlockSpec((rows, features), lambda i, p: (0, p[i])),
        ),
        out_shape=jax.ShapeDtypeStruct((rows, blocks * features), jnp.bfloat16),
        compiler_params=pltpu.CompilerParams(vmem_limit_bytes=16 * 1024 * 1024),
        cost_estimate=pl.CostEstimate(
            flops=4 * rows * columns * blocks * features, bytes_accessed=4 * own_weight.size, transcendentals=0
        ),
        name="project",
    )(place, own, other, own_weight, other_weight)


def attention_block(queries, key_rows, value_rows, out_weight):
    size = lax.axis_size("seq")
    depth = size // 2
    z, y = lax.axis_index("seq") // 2, lax.axis_index("seq") % 2
    rows = queries.shape[0]
    columns = queries.shape[1] // depth
    per_group = queries.shape[1] // key_rows.shape[1] * HD

    def heads_of(array, step):
        return lax.dynamic_slice_in_dim(array, (z + step) % depth * columns, columns, axis=1)

    def keyed_of(step):
        start = (z + step) % depth * columns // per_group * HD
        return [lax.dynamic_slice_in_dim(array, start, HD, axis=1) for array in (key_rows, value_rows)]

    steps = sorted(range(1, depth), key=lambda d: -min(d, depth - d))
    message = {0: jnp.concatenate([heads_of(queries, 0)] + keyed_of(0), axis=1)}
    for d in steps:
        sent = jnp.concatenate([heads_of(queries, d)] + keyed_of(d), axis=1)
        message[d] = lax.ppermute(sent, "seq", ring(size, d))
    keyed = {d: message[d][:, columns:] for d in message}
    across = {d: lax.ppermute(keyed[d], "seq", swap(size)) for d in [0] + steps}
    weight = {0: heads_of(out_weight, 0)}
    for d in steps:
        weight[d] = lax.ppermute(heads_of(out_weight, d), "seq", ring(size, d))
    weight_across = {d: lax.ppermute(weight[d], "seq", swap(size)) for d in [0] + steps}

    behind = (z - jnp.arange(depth, dtype=jnp.int32)) % depth
    block = (behind[:, None] * 2 + jnp.stack([y, 1 - y])[None, :]).astype(jnp.int32)
    key_pos = (block.reshape(-1, 1) * rows + jnp.arange(rows, dtype=jnp.int32)).reshape(1, -1)
    context = attend(
        block[:, 0] * rows,
        key_pos,
        jnp.stack([message[d][:, :columns] for d in range(depth)]),
        jnp.concatenate([part for d in range(depth) for part in (keyed[d], across[d])]),
    )
    halves = context.reshape(depth, 2, rows // 2, columns)
    core = lax.axis_index("exp")
    own = lax.dynamic_index_in_dim(halves, core, 1, keepdims=False).reshape(-1, columns)
    given = lax.dynamic_index_in_dim(halves, 1 - core, 1, keepdims=False).reshape(-1, columns)
    other = lax.ppermute(given, "exp", swap(2))

    own_weight = jnp.stack([part for d in range(depth) for part in (weight[d], weight_across[d])])
    other_weight = lax.ppermute(own_weight, "exp", swap(2))
    partial = project(block.reshape(-1), own, other, own_weight, other_weight)
    partial = partial.reshape(depth, rows // 2, -1)
    total = wide(partial[0])
    for d in steps:
        total = total + wide(lax.ppermute(partial[d], "seq", ring(size, -d)))
    return total


def gather_meta(meta, size, depth):
    along = jnp.stack([meta] + [lax.ppermute(meta, "seq", ring(size, d)) for d in range(1, depth)])
    both = jnp.stack([along, lax.ppermute(along, "seq", swap(size))], axis=1)
    return jnp.stack([both, lax.ppermute(both, "exp", swap(2))], axis=2)


def routing(ids, gates, first, local_experts):
    blocks, rows, _ = ids.shape
    subs = blocks // 4
    experts = first + jnp.arange(local_experts, dtype=jnp.int32)
    match = ids[..., None] == experts
    hit = jnp.any(match, axis=2)
    weight = jnp.sum(jnp.where(match, gates[..., None], 0.0), axis=2)
    count = hit.astype(jnp.int32)
    place = jnp.where(hit, jnp.cumsum(count, axis=1) - count, -1)
    place = place.reshape(subs, 4, rows, local_experts).transpose(3, 0, 1, 2)
    weight = weight.reshape(subs, 4, rows, local_experts).transpose(3, 0, 1, 2)
    chosen = place[:, :, :, None, :] == jnp.arange(CAP, dtype=jnp.int32)[:, None]
    row_gate = jnp.sum(jnp.where(chosen, weight[:, :, :, None, :], 0.0), axis=-1)
    row_gate = row_gate.reshape(local_experts, subs * 4 * CAP, 1)
    diagonal = jnp.eye(4, dtype=bool)[:, None, :, None]
    full = chosen[:, :, :, :, None, :] & diagonal
    select = full.reshape(local_experts, subs, 4 * CAP, 4 * rows).astype(jnp.bfloat16)
    spread = select.transpose(1, 3, 0, 2).reshape(subs, 4 * rows, local_experts * 4 * CAP)
    return select, spread, row_gate


def expert_kernel(x_ref, select_ref, spread_ref, gate_ref, wg_ref, wu_ref, wo_ref, out_ref, xg, acc, res):
    expert, chunk = pl.program_id(0), pl.program_id(1)
    last = pl.num_programs(1) - 1
    subs, slots = select_ref.shape[1], select_ref.shape[2]
    tokens = x_ref.shape[1]

    @pl.when(chunk == 0)
    def _():
        for s in range(subs):
            xg[s * slots : (s + 1) * slots, :] = jnp.dot(
                select_ref[expert, s], x_ref[s], preferred_element_type=jnp.float32
            ).astype(jnp.bfloat16)

    rows = xg[...]
    gate = jnp.dot(rows, wg_ref[0], preferred_element_type=jnp.float32)
    up = jnp.dot(rows, wu_ref[0], preferred_element_type=jnp.float32)
    act = (gate / (1.0 + jnp.exp(-gate)) * up).astype(jnp.bfloat16)
    part = jnp.dot(act, wo_ref[0], preferred_element_type=jnp.float32)

    @pl.when(chunk == 0)
    def _():
        acc[...] = part

    @pl.when(chunk > 0)
    def _():
        acc[...] += part

    @pl.when(chunk == last)
    def _():
        scaled = (acc[...] * gate_ref[expert]).astype(jnp.bfloat16)
        for s in range(subs):
            res[s, expert] = scaled[s * slots : (s + 1) * slots, :]

    @pl.when((chunk == last) & (expert == pl.num_programs(0) - 1))
    def _():
        for s in range(subs):
            out_ref[s * tokens : (s + 1) * tokens, :] = jnp.dot(
                spread_ref[s], res[s].reshape(-1, res.shape[-1]), preferred_element_type=jnp.float32
            ).astype(jnp.bfloat16)


def run_experts(x, select, spread, row_gate, expert_in, expert_out):
    subs, tokens, width = x.shape
    local_experts, hidden, _ = expert_out.shape
    slots = select.shape[2]
    chunks = hidden // FCHUNK
    flops = local_experts * subs * slots * width * hidden * 6
    moved = (expert_in.size + expert_out.size + 2 * x.size) * 2
    whole = lambda shape: pl.BlockSpec(shape, lambda e, f: (0,) * len(shape), pipeline_mode=pl.Buffered(1))
    return pl.pallas_call(
        expert_kernel,
        grid=(local_experts, chunks),
        out_shape=jax.ShapeDtypeStruct((subs * tokens, width), jnp.bfloat16),
        in_specs=[
            whole(x.shape),
            whole(select.shape),
            whole(spread.shape),
            whole(row_gate.shape),
            pl.BlockSpec((1, width, FCHUNK), lambda e, f: (e, 0, f)),
            pl.BlockSpec((1, width, FCHUNK), lambda e, f: (e, 0, f + chunks)),
            pl.BlockSpec((1, FCHUNK, width), lambda e, f: (e, f, 0)),
        ],
        out_specs=whole((subs * tokens, width)),
        scratch_shapes=[
            pltpu.VMEM((subs * slots, width), jnp.bfloat16),
            pltpu.VMEM((subs * slots, width), jnp.float32),
            pltpu.VMEM((subs, local_experts, slots, width), jnp.bfloat16),
        ],
        compiler_params=pltpu.CompilerParams(vmem_limit_bytes=48 * 1024 * 1024),
        cost_estimate=pl.CostEstimate(flops=flops, bytes_accessed=moved, transcendentals=0),
        name="experts",
    )(x, select, spread, row_gate, expert_in, expert_in, expert_out)


def expert_block(mixed, norm_gain, expert_ids, gate_weights, expert_in, expert_out):
    size = lax.axis_size("seq")
    depth = size // 2
    rows, width = mixed.shape
    local_experts = expert_in.shape[0]
    first = (lax.axis_index("seq") * 2 + lax.axis_index("exp")) * local_experts
    gate_high = gate_weights.astype(jnp.bfloat16)
    gate_low = (gate_weights - wide(gate_high)).astype(jnp.bfloat16)
    meta = jnp.concatenate([expert_ids.astype(jnp.bfloat16), gate_high, gate_low], axis=1)
    meta = gather_meta(meta, size, depth)
    top = expert_ids.shape[1]
    passes = [list(range(depth // 2)), list(range(depth // 2, depth))]
    routes = []
    for group in passes:
        own = meta[group[0] : group[-1] + 1].transpose(2, 0, 1, 3, 4).reshape(-1, rows, 3 * top)
        ids = own[..., :top].astype(jnp.int32)
        gates = wide(own[..., top : 2 * top]) + wide(own[..., 2 * top :])
        routes.append(routing(ids, gates, first, local_experts))

    normed = (
        mixed * lax.rsqrt(jnp.mean(mixed * mixed, axis=-1, keepdims=True) + 1e-06) * norm_gain
    ).astype(jnp.bfloat16)
    along, across = [normed], []
    for d in range(depth):
        if d + 1 < depth:
            along.append(lax.ppermute(along[d], "seq", ring(size, 1)))
        across.append(lax.ppermute(along[d], "seq", swap(size)))
    total = mixed
    for group, route in zip(passes, routes):
        mine = jnp.concatenate([part for d in group for part in (along[d], across[d])])
        other = lax.ppermute(mine, "exp", swap(2))
        x = jnp.concatenate([mine, other]).reshape(-1, 4 * rows, width)
        out = run_experts(x, *route, expert_in, expert_out).reshape(2, len(group), 2, rows, width)
        arrived = lax.ppermute(out[1], "exp", swap(2))
        pair = wide(out[0]) + wide(arrived)
        for place, d in enumerate(group):
            there = lax.ppermute(pair[place, 1].astype(jnp.bfloat16), "seq", swap(size))
            chip = pair[place, 0] + wide(there)
            if d:
                chip = wide(lax.ppermute(chip.astype(jnp.bfloat16), "seq", ring(size, -d)))
            total = total + chip
    return total.astype(jnp.bfloat16)


def on_device(
    stream,
    queries,
    key_rows,
    value_rows,
    out_weight,
    norm_gain,
    expert_ids,
    gate_weights,
    expert_in,
    expert_out,
):
    attn_out = attention_block(queries, key_rows, value_rows, out_weight)
    mixed = wide(stream) + attn_out
    return expert_block(mixed, norm_gain, expert_ids, gate_weights, expert_in, expert_out)


def solution(mesh):
    in_specs = (
        P(("groups", "seq", "exp"), None),
        P(("groups", "seq"), "exp"),
        P(("groups", "seq"), "exp"),
        P(("groups", "seq"), "exp"),
        P("seq", "exp"),
        P(),
        P(("groups", "seq", "exp"), None),
        P(("groups", "seq", "exp"), None),
        P(("seq", "exp"), None, None),
        P(("seq", "exp"), None, None),
    )
    out_specs = P(("groups", "seq", "exp"), None)
    return jax.shard_map(
        on_device, mesh=mesh, in_specs=in_specs, out_specs=out_specs, check_vma=False
    )
```

```python
import jax
import jax.numpy as jnp
from jax import lax
from jax.experimental import pallas as pl
from jax.experimental.pallas import tpu as pltpu
from jax.sharding import PartitionSpec as P

HD = 128
CAP = 12

neg_large = -1e30
smem = pl.BlockSpec(memory_space=pltpu.SMEM)
vmem = pl.BlockSpec(memory_space=pltpu.VMEM)


def limit(mebibytes):
    return pltpu.CompilerParams(vmem_limit_bytes=mebibytes * 1024 * 1024)


def ring(size, step):
    return [(i, (i + 2 * step) % size) for i in range(size)]


def swap(size):
    return [(i, i ^ 1) for i in range(size)]


def far_first(depth):
    return sorted(range(1, depth), key=lambda d: -min(d, depth - d))


def wide(value):
    return value.astype(jnp.float32)


def narrow(value):
    return value.astype(jnp.bfloat16)


def after(value, *others):
    return lax.optimization_barrier((value,) + others)[0]


def pack_heads(z, queries, key_rows, value_rows, depth):
    rows = queries.shape[0]
    columns = queries.shape[1] // depth
    per_group = queries.shape[1] // key_rows.shape[1] * HD

    def kernel(z_ref, query_ref, key_ref, value_ref, *out_refs):
        for d, out_ref in enumerate(out_refs):
            start = (z_ref[0] + d) % depth * columns
            group = pl.ds(pl.multiple_of(start // per_group * HD, HD), HD)
            out_ref[:, :columns] = query_ref[:, pl.ds(pl.multiple_of(start, HD), columns)]
            out_ref[:, columns : columns + HD] = key_ref[:, group]
            out_ref[:, columns + HD :] = value_ref[:, group]

    return pl.pallas_call(
        kernel,
        out_shape=[jax.ShapeDtypeStruct((rows, columns + 2 * HD), queries.dtype)] * depth,
        in_specs=[smem, vmem, vmem, vmem],
        out_specs=[vmem] * depth,
        compiler_params=limit(16),
        name="pack_heads",
    )(z, queries, key_rows, value_rows)


def pack_weight(z, out_weight, depth):
    rows = out_weight.shape[0]
    columns = out_weight.shape[1] // depth

    def kernel(z_ref, weight_ref, *out_refs):
        for d, out_ref in enumerate(out_refs):
            start = pl.multiple_of((z_ref[0] + d) % depth * columns, HD)
            out_ref[...] = weight_ref[:, pl.ds(start, columns)]

    return pl.pallas_call(
        kernel,
        out_shape=[jax.ShapeDtypeStruct((rows, columns), out_weight.dtype)] * depth,
        in_specs=[smem, vmem],
        out_specs=[vmem] * depth,
        compiler_params=limit(16),
        name="pack_weight",
    )(z, out_weight)


def attend(core, starts, key_pos, messages, across, columns):
    depth = len(messages)
    rows = messages[0].shape[0]
    heads = columns // HD
    length = 2 * depth * rows
    half = rows // 2

    def kernel(core_ref, starts_ref, key_pos_ref, *refs):
        message_refs, across_refs = refs[:depth], refs[depth : 2 * depth]
        out_ref, query, keyed = refs[2 * depth :]
        for d in range(depth):
            for h in range(heads):
                query[d, h * rows : (h + 1) * rows, :] = message_refs[d][:, h * HD : (h + 1) * HD]
            keyed[2 * d * rows : (2 * d + 1) * rows, :] = message_refs[d][:, columns:]
            keyed[(2 * d + 1) * rows : (2 * d + 2) * rows, :] = across_refs[d][...]
        mine = core_ref[0] == 0

        def block(d, carry):
            scores = lax.dot_general(
                query[d], keyed[:, :HD], (((1,), (1,)), ((), ())), preferred_element_type=jnp.float32
            )
            offset = lax.broadcasted_iota(jnp.int32, (heads * rows, 1), 0) % rows
            allowed = key_pos_ref[...] <= starts_ref[d] + offset
            scores = jnp.where(allowed, scores, neg_large)
            largest = jnp.max(scores, axis=-1, keepdims=True)
            exps = jnp.exp((scores - largest) * (HD**-0.5))
            total = jnp.sum(exps, axis=-1, keepdims=True)
            summed = jnp.dot(narrow(exps), keyed[:, HD:], preferred_element_type=jnp.float32)
            context = narrow(summed / total)
            place = pl.ds(pl.multiple_of(d * half, half), half)
            for h in range(heads):
                low, high = context[h * rows : h * rows + half], context[h * rows + half : (h + 1) * rows]
                out_ref[0, place, h * HD : (h + 1) * HD] = jnp.where(mine, low, high)
                out_ref[1, place, h * HD : (h + 1) * HD] = jnp.where(mine, high, low)
            return carry

        lax.fori_loop(0, depth, block, 0)

    work = depth * rows * columns * length
    return pl.pallas_call(
        kernel,
        out_shape=jax.ShapeDtypeStruct((2, depth * half, columns), jnp.bfloat16),
        in_specs=[smem, smem, vmem] + [vmem] * (2 * depth),
        out_specs=vmem,
        scratch_shapes=[
            pltpu.VMEM((depth, heads * rows, HD), jnp.bfloat16),
            pltpu.VMEM((length, 2 * HD), jnp.bfloat16),
        ],
        compiler_params=limit(32),
        cost_estimate=pl.CostEstimate(flops=4 * work, bytes_accessed=depth * rows * columns * 8, transcendentals=work // HD),
        name="attend",
    )(core, starts, key_pos, *messages, *across)


def project(place, context, weights):
    rows, columns = context.shape[1:]
    blocks, features = len(weights), weights[0].shape[0]
    if features % HD:
        weight = jnp.stack(weights)[jnp.argsort(place)]
        result = jnp.einsum("erc,bfc->erbf", context, weight, preferred_element_type=jnp.float32)
        result = narrow(result.reshape(2, rows, -1))
        return result[0], result[1]

    def kernel(place_ref, context_ref, *refs):
        weight_refs, kept_ref, given_ref = refs[:blocks], refs[blocks], refs[blocks + 1]
        left = context_ref[...].reshape(2 * rows, columns)
        for i in range(blocks):
            part = narrow(
                lax.dot_general(
                    left, weight_refs[i][...], (((1,), (1,)), ((), ())), preferred_element_type=jnp.float32
                )
            )
            there = pl.ds(pl.multiple_of(place_ref[i] * features, HD), features)
            kept_ref[:, there] = part[:rows]
            given_ref[:, there] = part[rows:]

    return pl.pallas_call(
        kernel,
        out_shape=[jax.ShapeDtypeStruct((rows, blocks * features), jnp.bfloat16)] * 2,
        in_specs=[smem, vmem] + [vmem] * blocks,
        out_specs=[vmem, vmem],
        compiler_params=limit(24),
        cost_estimate=pl.CostEstimate(
            flops=4 * rows * columns * blocks * features,
            bytes_accessed=2 * blocks * features * (columns + 2 * rows),
            transcendentals=0,
        ),
        name="project",
    )(place, context, *weights)


def attention_block(queries, key_rows, value_rows, out_weight):
    size = lax.axis_size("seq")
    depth = size // 2
    z, y = lax.axis_index("seq") // 2, lax.axis_index("seq") % 2
    core = lax.axis_index("exp").astype(jnp.int32).reshape(1)
    rows = queries.shape[0]
    columns = queries.shape[1] // depth
    steps = far_first(depth)
    here = z.astype(jnp.int32).reshape(1)

    message = list(pack_heads(here, queries, key_rows, value_rows, depth))
    for d in steps:
        message[d] = lax.ppermute(message[d], "seq", ring(size, d))
    across = {}
    for d in [0] + steps:
        across[d] = lax.ppermute(message[d][:, columns:], "seq", swap(size))
    weight = list(pack_weight(here, out_weight, depth))
    weight_across = {0: lax.ppermute(weight[0], "seq", swap(size))}
    for d in steps[::-1]:
        weight[d] = lax.ppermute(after(weight[d], *message), "seq", ring(size, d))

    behind = (z - jnp.arange(depth, dtype=jnp.int32)) % depth
    block = (behind[:, None] * 2 + jnp.stack([y, 1 - y])[None, :]).astype(jnp.int32)
    key_pos = (block.reshape(-1, 1) * rows + jnp.arange(rows, dtype=jnp.int32)).reshape(1, -1)
    context = attend(core, block[:, 0] * rows, key_pos, message, [across[d] for d in range(depth)], columns)
    for d in steps[::-1]:
        weight_across[d] = lax.ppermute(weight[d], "seq", swap(size))
    kept, given = project(
        block.reshape(-1), context, [part for d in range(depth) for part in (weight[d], weight_across[d])]
    )
    arrived = lax.ppermute(given, "exp", swap(2))
    chip = (wide(kept) + wide(arrived)).reshape(depth, rows // 2, -1)
    total = chip[0]
    for d in steps:
        total = total + wide(lax.ppermute(narrow(chip[d]), "seq", ring(size, -d)))
    return total, message[steps[-1]]


def gather_meta(meta, size, depth):
    along = jnp.stack([meta] + [lax.ppermute(meta, "seq", ring(size, d)) for d in range(1, depth)])
    both = jnp.stack([along, lax.ppermute(along, "seq", swap(size))], axis=1)
    return jnp.stack([both, lax.ppermute(both, "exp", swap(2))], axis=1)


def routing(ids, gates, first, local_experts):
    subs, blocks, rows, _ = ids.shape
    experts = first + jnp.arange(local_experts, dtype=jnp.int32)
    match = ids[..., None] == experts
    hit = jnp.any(match, axis=3)
    weight = jnp.sum(jnp.where(match, gates[..., None], 0.0), axis=3)
    count = hit.astype(jnp.int32)
    place = jnp.where(hit, jnp.cumsum(count, axis=2) - count, -1)
    place = place.transpose(3, 0, 1, 2)
    weight = weight.transpose(3, 0, 1, 2)
    chosen = place[:, :, :, None, :] == jnp.arange(CAP, dtype=jnp.int32)[:, None]
    row_gate = jnp.sum(jnp.where(chosen, weight[:, :, :, None, :], 0.0), axis=-1)
    row_gate = row_gate.reshape(local_experts, subs * blocks * CAP, 1)
    diagonal = jnp.eye(blocks, dtype=bool)[:, None, :, None]
    full = chosen[:, :, :, :, None, :] & diagonal
    select = full.reshape(local_experts, subs, blocks * CAP, blocks * rows).astype(jnp.bfloat16)
    spread = select.transpose(1, 3, 0, 2).reshape(subs, blocks * rows, local_experts * blocks * CAP)
    return select, spread, row_gate


def run_experts(mine, other, select, spread, row_gate, expert_in, expert_out):
    subs = len(mine)
    tokens, width = mine[0].shape
    local_experts, hidden, _ = expert_out.shape
    slots = select.shape[2]

    def kernel(select_ref, spread_ref, gate_ref, wg_ref, wu_ref, wo_ref, *refs):
        mine_refs, other_refs = refs[:subs], refs[subs : 2 * subs]
        kept_refs, given_refs = refs[2 * subs : 3 * subs], refs[3 * subs : 4 * subs]
        xg, res = refs[4 * subs :]
        expert = pl.program_id(0)
        for s in range(subs):
            xg[s * slots : (s + 1) * slots, :] = narrow(
                jnp.dot(select_ref[expert, s, :, :tokens], mine_refs[s][...], preferred_element_type=jnp.float32)
                + jnp.dot(select_ref[expert, s, :, tokens:], other_refs[s][...], preferred_element_type=jnp.float32)
            )
        rows = xg[...]
        gate = jnp.dot(rows, wg_ref[0], preferred_element_type=jnp.float32)
        up = jnp.dot(rows, wu_ref[0], preferred_element_type=jnp.float32)
        act = narrow(gate / (1.0 + jnp.exp(-gate)) * up)
        part = jnp.dot(act, wo_ref[0], preferred_element_type=jnp.float32)
        scaled = narrow(part * gate_ref[expert])
        for s in range(subs):
            res[s, expert] = scaled[s * slots : (s + 1) * slots, :]

        @pl.when(expert == pl.num_programs(0) - 1)
        def _():
            for s in range(subs):
                both = narrow(
                    jnp.dot(spread_ref[s], res[s].reshape(-1, width), preferred_element_type=jnp.float32)
                )
                kept_refs[s][...] = both[:tokens]
                given_refs[s][...] = both[tokens:]

    flops = local_experts * subs * slots * width * hidden * 6
    moved = (expert_in.size + expert_out.size + 8 * subs * tokens * width) * 2

    def whole(shape):
        return pl.BlockSpec(shape, lambda e: (0,) * len(shape), pipeline_mode=pl.Buffered(1))

    piece = whole((tokens, width))
    outs = pl.pallas_call(
        kernel,
        grid=(local_experts,),
        out_shape=[jax.ShapeDtypeStruct((tokens, width), jnp.bfloat16)] * (2 * subs),
        in_specs=[
            whole(select.shape),
            whole(spread.shape),
            whole(row_gate.shape),
            pl.BlockSpec((1, width, hidden), lambda e: (e, 0, 0)),
            pl.BlockSpec((1, width, hidden), lambda e: (e, 0, 1)),
            pl.BlockSpec((1, hidden, width), lambda e: (e, 0, 0)),
        ]
        + [piece] * (2 * subs),
        out_specs=[piece] * (2 * subs),
        scratch_shapes=[
            pltpu.VMEM((subs * slots, width), jnp.bfloat16),
            pltpu.VMEM((subs, local_experts, slots, width), jnp.bfloat16),
        ],
        compiler_params=limit(56),
        cost_estimate=pl.CostEstimate(flops=flops, bytes_accessed=moved, transcendentals=0),
        name="experts",
    )(select, spread, row_gate, expert_in, expert_in, expert_out, *mine, *other)
    return outs[:subs], outs[subs:]


def expert_block(mixed, early, norm_gain, expert_ids, gate_weights, expert_in, expert_out):
    size = lax.axis_size("seq")
    depth = size // 2
    rows, width = mixed.shape
    local_experts = expert_in.shape[0]
    top = expert_ids.shape[1]
    first = (lax.axis_index("seq") * 2 + lax.axis_index("exp")) * local_experts
    gate_high = narrow(gate_weights)
    gate_low = narrow(gate_weights - wide(gate_high))
    meta = jnp.concatenate([narrow(expert_ids), gate_high, gate_low], axis=1)
    meta = gather_meta(after(meta, early), size, depth).reshape(depth, 4, rows, 3 * top)
    ids = meta[..., :top].astype(jnp.int32)
    gates = wide(meta[..., top : 2 * top]) + wide(meta[..., 2 * top :])
    route = routing(ids, gates, first, local_experts)

    normed = narrow(mixed * lax.rsqrt(jnp.mean(mixed * mixed, axis=-1, keepdims=True) + 1e-06) * norm_gain)
    along, mine, other = [normed], [], []
    for d in range(depth):
        if d + 1 < depth:
            along.append(lax.ppermute(along[d], "seq", ring(size, 1)))
        mine.append(jnp.concatenate([along[d], lax.ppermute(along[d], "seq", swap(size))]))
        other.append(lax.ppermute(mine[d], "exp", swap(2)))
    kept, given = run_experts(mine, other, *route, expert_in, expert_out)

    total = mixed
    for d in far_first(depth) + [0]:
        pair = wide(kept[d]) + wide(lax.ppermute(given[d], "exp", swap(2)))
        there = lax.ppermute(narrow(pair[rows:]), "seq", swap(size))
        chip = pair[:rows] + wide(there)
        if d:
            chip = wide(lax.ppermute(narrow(chip), "seq", ring(size, -d)))
        total = total + chip
    return narrow(total)


def on_device(
    stream,
    queries,
    key_rows,
    value_rows,
    out_weight,
    norm_gain,
    expert_ids,
    gate_weights,
    expert_in,
    expert_out,
):
    attn_out, early = attention_block(queries, key_rows, value_rows, out_weight)
    mixed = wide(stream) + attn_out
    return expert_block(mixed, early, norm_gain, expert_ids, gate_weights, expert_in, expert_out)


def solution(mesh):
    in_specs = (
        P(("groups", "seq", "exp"), None),
        P(("groups", "seq"), "exp"),
        P(("groups", "seq"), "exp"),
        P(("groups", "seq"), "exp"),
        P("seq", "exp"),
        P(),
        P(("groups", "seq", "exp"), None),
        P(("groups", "seq", "exp"), None),
        P(("seq", "exp"), None, None),
        P(("seq", "exp"), None, None),
    )
    out_specs = P(("groups", "seq", "exp"), None)
    return jax.shard_map(
        on_device, mesh=mesh, in_specs=in_specs, out_specs=out_specs, check_vma=False
    )
```

```python
import jax
import jax.numpy as jnp
from jax import lax
from jax.experimental import pallas as pl
from jax.experimental.pallas import tpu as pltpu
from jax.sharding import PartitionSpec as P

HD = 128
CAP = 12

neg_large = -1e30
smem = pl.BlockSpec(memory_space=pltpu.SMEM)
vmem = pl.BlockSpec(memory_space=pltpu.VMEM)
unread = pl.BlockSpec(memory_space=pl.ANY)


def limit(mebibytes):
    return pltpu.CompilerParams(vmem_limit_bytes=mebibytes * 1024 * 1024)


def ring(size, step):
    return [(i, (i + 2 * step) % size) for i in range(size)]


def swap(size):
    return [(i, i ^ 1) for i in range(size)]


def far_first(depth):
    return sorted(range(1, depth), key=lambda d: -min(d, depth - d))


def wide(value):
    return value.astype(jnp.float32)


def narrow(value):
    return value.astype(jnp.bfloat16)


def pack_heads(z, queries, key_rows, value_rows, out_weight, expert_ids, gate_weights, depth):
    rows = queries.shape[0]
    columns = queries.shape[1] // depth
    per_group = queries.shape[1] // key_rows.shape[1] * HD
    tokens, top = expert_ids.shape
    lines = tokens // 4

    def kernel(z_ref, query_ref, key_ref, value_ref, weight_ref, id_ref, gate_ref, *out_refs):
        gates = gate_ref[...]
        high = wide(narrow(gates))
        blank = jnp.zeros((tokens, HD // 2 - 3 * top), jnp.float32)
        meta = jnp.concatenate([wide(id_ref[...]), high, gates - high, blank], axis=1)
        meta = jnp.concatenate([meta[g * lines : (g + 1) * lines] for g in range(4)], axis=1)
        for d, out_ref in enumerate(out_refs[:depth]):
            start = (z_ref[0] + d) % depth * columns
            group = pl.ds(pl.multiple_of(start // per_group * HD, HD), HD)
            out_ref[:rows, :columns] = query_ref[:, pl.ds(pl.multiple_of(start, HD), columns)]
            out_ref[:rows, columns : columns + HD] = key_ref[:, group]
            out_ref[:rows, columns + HD :] = value_ref[:, group]
            out_ref[rows:, :columns] = jnp.zeros((lines, columns), jnp.bfloat16)
            out_ref[rows:, columns:] = narrow(meta)
        out_refs[depth][...] = weight_ref[:, pl.ds(pl.multiple_of(z_ref[0] * columns, HD), columns)]

    return pl.pallas_call(
        kernel,
        out_shape=[jax.ShapeDtypeStruct((rows + lines, columns + 2 * HD), queries.dtype)] * depth
        + [jax.ShapeDtypeStruct((out_weight.shape[0], columns), out_weight.dtype)],
        in_specs=[smem] + [vmem] * 6,
        out_specs=[vmem] * (depth + 1),
        compiler_params=limit(16),
        name="pack_heads",
    )(z, queries, key_rows, value_rows, out_weight, expert_ids, gate_weights)


def pack_weight(z, out_weight, depth, before):
    rows = out_weight.shape[0]
    columns = out_weight.shape[1] // depth

    def kernel(z_ref, weight_ref, *refs):
        for d, out_ref in enumerate(refs[len(before) :]):
            start = pl.multiple_of((z_ref[0] + d + 1) % depth * columns, HD)
            out_ref[...] = weight_ref[:, pl.ds(start, columns)]

    return pl.pallas_call(
        kernel,
        out_shape=[jax.ShapeDtypeStruct((rows, columns), out_weight.dtype)] * (depth - 1),
        in_specs=[smem, vmem] + [unread] * len(before),
        out_specs=[vmem] * (depth - 1),
        compiler_params=limit(16),
        name="pack_weight",
    )(z, out_weight, *before)


def collect_meta(near, across, rows):
    lines = across[0].shape[0] - rows
    parts = [part for pair in zip(near, across) for part in pair]

    def kernel(*refs):
        for i, ref in enumerate(refs[:-1]):
            refs[-1][i * lines : (i + 1) * lines, :] = ref[rows:, -2 * HD :]

    return pl.pallas_call(
        kernel,
        out_shape=jax.ShapeDtypeStruct((len(parts) * lines, 2 * HD), jnp.bfloat16),
        in_specs=[vmem] * len(parts),
        out_specs=vmem,
        compiler_params=limit(16),
        name="collect_meta",
    )(*parts)


def attend(core, starts, key_pos, messages, across, rows, columns):
    depth = len(messages)
    heads = columns // HD
    length = 2 * depth * rows
    half = rows // 2

    def kernel(core_ref, starts_ref, key_pos_ref, *refs):
        message_refs, across_refs = refs[:depth], refs[depth : 2 * depth]
        out_refs, (query, keyed) = refs[-2 - depth : -2], refs[-2:]
        for d in range(depth):
            for h in range(heads):
                query[d, h * rows : (h + 1) * rows, :] = message_refs[d][:rows, h * HD : (h + 1) * HD]
            keyed[2 * d * rows : (2 * d + 1) * rows, :] = message_refs[d][:rows, columns:]
            keyed[(2 * d + 1) * rows : (2 * d + 2) * rows, :] = across_refs[d][:rows, :]
        mine = core_ref[0] == 0

        for d in range(depth):
            scores = lax.dot_general(
                query[d], keyed[:, :HD], (((1,), (1,)), ((), ())), preferred_element_type=jnp.float32
            )
            offset = lax.broadcasted_iota(jnp.int32, (heads * rows, 1), 0) % rows
            allowed = key_pos_ref[...] <= starts_ref[d] + offset
            scores = jnp.where(allowed, scores, neg_large)
            largest = jnp.max(scores, axis=-1, keepdims=True)
            exps = jnp.exp((scores - largest) * (HD**-0.5))
            total = jnp.sum(exps, axis=-1, keepdims=True)
            summed = jnp.dot(narrow(exps), keyed[:, HD:], preferred_element_type=jnp.float32)
            context = narrow(summed / total)
            for h in range(heads):
                low, high = context[h * rows : h * rows + half], context[h * rows + half : (h + 1) * rows]
                out_refs[d][:half, h * HD : (h + 1) * HD] = jnp.where(mine, low, high)
                out_refs[d][half:, h * HD : (h + 1) * HD] = jnp.where(mine, high, low)

    work = depth * rows * columns * length
    return pl.pallas_call(
        kernel,
        out_shape=[jax.ShapeDtypeStruct((rows, columns), jnp.bfloat16)] * depth,
        in_specs=[smem, smem, vmem] + [vmem] * (2 * depth),
        out_specs=[vmem] * depth,
        scratch_shapes=[
            pltpu.VMEM((depth, heads * rows, HD), jnp.bfloat16),
            pltpu.VMEM((length, 2 * HD), jnp.bfloat16),
        ],
        compiler_params=limit(24),
        cost_estimate=pl.CostEstimate(flops=160 * work, bytes_accessed=depth * rows * columns * 8, transcendentals=work // HD),
        name="attend",
    )(core, starts, key_pos, *messages, *across)


def project(place, context, weights, before):
    depth, blocks = len(context), len(weights)
    rows, columns = context[0].shape[0] // 2, context[0].shape[1]
    features = weights[0].shape[0]
    shape = (depth, rows, blocks * features)
    if features % HD:
        weight = jnp.stack(weights)[jnp.argsort(place)]
        left = jnp.stack(context).reshape(depth, 2, rows, columns)
        result = jnp.einsum("dcrk,bfk->cdrbf", left, weight, preferred_element_type=jnp.float32)
        result = narrow(result.reshape((2,) + shape))
        return result[0], result[1]

    def kernel(place_ref, *refs):
        context_refs, weight_refs, out_refs = refs[:depth], refs[depth : depth + blocks], refs[-3:-1]
        left_ref = refs[-1]
        for d in range(depth):
            left_ref[2 * d * rows : 2 * (d + 1) * rows, :] = context_refs[d][...]
        left = left_ref[...]
        for i in range(blocks):
            part = narrow(
                lax.dot_general(
                    left, weight_refs[i][...], (((1,), (1,)), ((), ())), preferred_element_type=jnp.float32
                )
            ).reshape(depth, 2, rows, features)
            there = pl.ds(pl.multiple_of(place_ref[i] * features, HD), features)
            for core in range(2):
                out_refs[core][:, :, there] = part[:, core]

    return pl.pallas_call(
        kernel,
        out_shape=[jax.ShapeDtypeStruct(shape, jnp.bfloat16)] * 2,
        in_specs=[smem] + [vmem] * (depth + blocks) + [unread] * len(before),
        out_specs=[vmem, vmem],
        scratch_shapes=[pltpu.VMEM((2 * depth * rows, columns), jnp.bfloat16)],
        compiler_params=limit(20),
        cost_estimate=pl.CostEstimate(
            flops=4 * depth * rows * columns * blocks * features,
            bytes_accessed=2 * blocks * features * columns + 4 * depth * rows * (columns + 2 * blocks * features),
            transcendentals=0,
        ),
        name="project",
    )(place, *context, *weights, *before)


def add_up(parts):
    def kernel(*refs):
        total = wide(refs[0][...])
        for ref in refs[1 : len(parts)]:
            total = total + wide(ref[...])
        refs[-2][...] = total
        refs[-1][...] = narrow(total)

    return pl.pallas_call(
        kernel,
        out_shape=[
            jax.ShapeDtypeStruct(parts[0].shape, jnp.float32),
            jax.ShapeDtypeStruct(parts[0].shape, jnp.bfloat16),
        ],
        in_specs=[vmem] * len(parts),
        out_specs=[vmem, vmem],
        compiler_params=limit(32),
        name="add_up",
    )(*parts)


def attention_block(stream, queries, key_rows, value_rows, out_weight, expert_ids, gate_weights, local_experts):
    size = lax.axis_size("seq")
    depth = size // 2
    z, y = lax.axis_index("seq") // 2, lax.axis_index("seq") % 2
    core = lax.axis_index("exp").astype(jnp.int32).reshape(1)
    rows = queries.shape[0]
    columns = queries.shape[1] // depth
    steps = far_first(depth)
    here = z.astype(jnp.int32).reshape(1)

    *message, own_weight = pack_heads(
        here, queries, key_rows, value_rows, out_weight, expert_ids, gate_weights, depth
    )
    for d in steps:
        message[d] = lax.ppermute(message[d], "seq", ring(size, d))
    across = {}
    for d in [0] + steps:
        across[d] = lax.ppermute(message[d][:, columns:], "seq", swap(size))
    across = [across[d] for d in range(depth)]
    weight = [own_weight] + list(pack_weight(here, out_weight, depth, [message[d] for d in steps]))
    weight_across = {0: lax.ppermute(own_weight, "seq", swap(size))}
    for d in steps[::-1]:
        weight[d] = lax.ppermute(weight[d], "seq", ring(size, d))
        weight_across[d] = lax.ppermute(weight[d], "seq", swap(size))
    first = (lax.axis_index("seq") * 2 + lax.axis_index("exp")) * local_experts
    meta = collect_meta(message, across, rows)
    meta = [meta, lax.ppermute(meta, "exp", swap(2))]
    route = routing(first, meta, depth, *expert_ids.shape, local_experts, [weight_across[0]])

    behind = (z - jnp.arange(depth, dtype=jnp.int32)) % depth
    block = (behind[:, None] * 2 + jnp.stack([y, 1 - y])[None, :]).astype(jnp.int32)
    key_pos = (block.reshape(-1, 1) * rows + jnp.arange(rows, dtype=jnp.int32)).reshape(1, -1)
    context = attend(core, block[:, 0] * rows, key_pos, message, across, rows, columns)
    kept, given = project(
        block.reshape(-1), context, [part for d in range(depth) for part in (weight[d], weight_across[d])], route[1:]
    )
    chip = wide(kept) + wide(lax.ppermute(given, "exp", swap(2)))
    parts = [stream, chip[0]]
    for d in steps:
        parts.append(lax.ppermute(narrow(chip[d]), "seq", ring(size, -d)))
    return *add_up(parts), route


def routing(first, meta, subs, rows, top, local_experts, before):
    lines = rows // 4
    tokens = 4 * rows
    slots = 4 * CAP
    lanes = 128
    contract = lambda a, b, i, j: lax.dot_general(a, b, (((i,), (j,)), ((), ())), preferred_element_type=jnp.float32)
    iota = lambda shape, axis: lax.broadcasted_iota(jnp.int32, shape, axis)

    def kernel(first_ref, mine_ref, other_ref, *refs):
        select_ref, spread_ref, gate_ref = refs[len(before) :]
        token, other = iota((tokens, tokens), 0), iota((tokens, tokens), 1)
        earlier = narrow(wide((other < token) & (other // rows == token // rows)))
        same = narrow(wide(token == other))
        lane = iota((tokens, lanes), 1)
        owner = narrow(wide(iota((lanes, local_experts * slots), 1) // slots == iota((lanes, local_experts * slots), 0)))
        slot = iota((local_experts * slots, tokens), 0)
        fits = slot % slots // CAP == iota((local_experts * slots, tokens), 1) // rows
        for s in range(subs):
            packed = []
            for ref in (mine_ref, other_ref):
                for y in range(2):
                    block = wide(ref[(2 * s + y) * lines : (2 * s + y + 1) * lines, :])
                    packed += [block[:, g * HD // 2 : g * HD // 2 + 3 * top] for g in range(4)]
            packed = jnp.concatenate(packed, axis=0)
            hit = jnp.zeros((tokens, lanes), jnp.float32)
            high, low = hit, hit
            for j in range(local_experts):
                match = packed[:, :top] == wide(first_ref[0] + j)
                column = lambda kind: jnp.sum(jnp.where(match, kind, 0.0), axis=1, keepdims=True)
                here = lane == j
                hit = jnp.where(here, column(1.0), hit)
                high = jnp.where(here, column(packed[:, top : 2 * top]), high)
                low = jnp.where(here, column(packed[:, 2 * top :]), low)
            place = contract(earlier, narrow(hit), 1, 0)
            by_slot = lambda value: contract(owner, narrow(value), 0, 1)
            chosen = (by_slot(hit) > 0.5) & (jnp.abs(by_slot(place) - wide(slot % CAP)) < 0.5) & fits
            gates = jnp.sum(jnp.where(chosen, by_slot(high) + by_slot(low), 0.0), axis=1, keepdims=True)
            chosen = narrow(wide(chosen))
            spread_ref[s] = narrow(contract(same, chosen, 1, 1))
            for j in range(local_experts):
                select_ref[j, s] = chosen[j * slots : (j + 1) * slots]
                gate_ref[j, s * slots : (s + 1) * slots, :] = gates[j * slots : (j + 1) * slots]

    return pl.pallas_call(
        kernel,
        out_shape=[
            jax.ShapeDtypeStruct((local_experts, subs, slots, tokens), jnp.bfloat16),
            jax.ShapeDtypeStruct((subs, tokens, local_experts * slots), jnp.bfloat16),
            jax.ShapeDtypeStruct((local_experts, subs * slots, 1), jnp.float32),
        ],
        in_specs=[smem, vmem, vmem] + [unread] * len(before),
        out_specs=[vmem] * 3,
        compiler_params=limit(32),
        name="routing",
    )(first.astype(jnp.int32).reshape(1), *meta, *before)


def run_experts(mine, other, select, spread, row_gate, norm_gain, expert_in, expert_out):
    subs = len(mine)
    tokens, width = mine[0].shape
    local_experts, hidden, _ = expert_out.shape
    slots = select.shape[2]

    def kernel(select_ref, spread_ref, gate_ref, gain_ref, wg_ref, wu_ref, wo_ref, *refs):
        mine_refs, other_refs = refs[:subs], refs[subs : 2 * subs]
        kept_refs, given_refs = refs[2 * subs : 3 * subs], refs[3 * subs : 4 * subs]
        xg, res = refs[4 * subs :]
        expert = pl.program_id(0)

        @pl.when(expert == 0)
        def _():
            for s in range(subs):
                choose = select_ref[:, s].reshape(local_experts * slots, 2 * tokens)
                picked = jnp.dot(
                    choose[:, :tokens], mine_refs[s][...], preferred_element_type=jnp.float32
                ) + jnp.dot(choose[:, tokens:], other_refs[s][...], preferred_element_type=jnp.float32)
                scale = lax.rsqrt(jnp.sum(picked * picked, axis=1, keepdims=True) * (1.0 / width) + 1e-06)
                rows = narrow(picked * scale * gain_ref[...])
                for e in range(local_experts):
                    xg[e, s * slots : (s + 1) * slots, :] = rows[e * slots : (e + 1) * slots]

        rows = xg[expert]
        gate = jnp.dot(rows, wg_ref[0], preferred_element_type=jnp.float32)
        up = jnp.dot(rows, wu_ref[0], preferred_element_type=jnp.float32)
        act = narrow(gate / (1.0 + jnp.exp(-gate)) * up)
        part_out = jnp.dot(act, wo_ref[0], preferred_element_type=jnp.float32)
        scaled = narrow(part_out * gate_ref[expert])
        for s in range(subs):
            res[s, expert] = scaled[s * slots : (s + 1) * slots, :]

        @pl.when(expert == pl.num_programs(0) - 1)
        def _():
            for s in range(subs):
                both = narrow(
                    jnp.dot(spread_ref[s], res[s].reshape(-1, width), preferred_element_type=jnp.float32)
                )
                kept_refs[s][...] = both[:tokens]
                given_refs[s][...] = both[tokens:]

    flops = local_experts * subs * slots * width * hidden * 6
    moved = (expert_in.size + expert_out.size + 8 * subs * tokens * width) * 2

    def whole(shape):
        return pl.BlockSpec(shape, lambda e: (0,) * len(shape), pipeline_mode=pl.Buffered(1))

    outs = pl.pallas_call(
        kernel,
        grid=(local_experts,),
        out_shape=[jax.ShapeDtypeStruct((tokens, width), jnp.bfloat16)] * (2 * subs),
        in_specs=[
            whole(select.shape),
            whole(spread.shape),
            whole(row_gate.shape),
            whole((1, width)),
            pl.BlockSpec((1, width, hidden), lambda e: (e, 0, 0)),
            pl.BlockSpec((1, width, hidden), lambda e: (e, 0, 1)),
            pl.BlockSpec((1, hidden, width), lambda e: (e, 0, 0)),
        ]
        + [whole((tokens, width))] * (2 * subs),
        out_specs=[whole((tokens, width))] * (2 * subs),
        scratch_shapes=[
            pltpu.VMEM((local_experts, subs * slots, width), jnp.bfloat16),
            pltpu.VMEM((subs, local_experts, slots, width), jnp.bfloat16),
        ],
        compiler_params=limit(34),
        cost_estimate=pl.CostEstimate(flops=flops, bytes_accessed=moved, transcendentals=0),
        name="experts",
    )(
        select,
        spread,
        row_gate,
        norm_gain.reshape(1, -1),
        expert_in,
        expert_in,
        expert_out,
        *mine,
        *other,
    )
    return outs[:subs], outs[subs:]


def expert_block(mixed, rounded, route, norm_gain, expert_in, expert_out):
    size = lax.axis_size("seq")
    depth = size // 2
    rows = mixed.shape[0]

    along, mine, other = [rounded], [], []
    for d in range(depth):
        if d + 1 < depth:
            along.append(lax.ppermute(along[d], "seq", ring(size, 1)))
        mine.append(jnp.concatenate([along[d], lax.ppermute(along[d], "seq", swap(size))]))
        other.append(lax.ppermute(mine[d], "exp", swap(2)))
    kept, given = run_experts(mine, other, *route, norm_gain, expert_in, expert_out)

    total = mixed
    for d in far_first(depth) + [0]:
        pair = wide(kept[d]) + wide(lax.ppermute(given[d], "exp", swap(2)))
        there = lax.ppermute(narrow(pair[rows:]), "seq", swap(size))
        chip = pair[:rows] + wide(there)
        if d:
            chip = wide(lax.ppermute(narrow(chip), "seq", ring(size, -d)))
        total = total + chip
    return narrow(total)


def on_device(
    stream,
    queries,
    key_rows,
    value_rows,
    out_weight,
    norm_gain,
    expert_ids,
    gate_weights,
    expert_in,
    expert_out,
):
    mixed, rounded, route = attention_block(
        stream, queries, key_rows, value_rows, out_weight, expert_ids, gate_weights, expert_in.shape[0]
    )
    return expert_block(mixed, rounded, route, norm_gain, expert_in, expert_out)


def solution(mesh):
    in_specs = (
        P(("groups", "seq", "exp"), None),
        P(("groups", "seq"), "exp"),
        P(("groups", "seq"), "exp"),
        P(("groups", "seq"), "exp"),
        P("seq", "exp"),
        P(),
        P(("groups", "seq", "exp"), None),
        P(("groups", "seq", "exp"), None),
        P(("seq", "exp"), None, None),
        P(("seq", "exp"), None, None),
    )
    out_specs = P(("groups", "seq", "exp"), None)
    return jax.shard_map(
        on_device, mesh=mesh, in_specs=in_specs, out_specs=out_specs, check_vma=False
    )
```

```python
import jax
import jax.numpy as jnp
from jax import lax
from jax.experimental import pallas as pl
from jax.experimental.pallas import tpu as pltpu
from jax.sharding import PartitionSpec as P

HD = 128
CAP = 12

neg_large = -1e30
smem = pl.BlockSpec(memory_space=pltpu.SMEM)
vmem = pl.BlockSpec(memory_space=pltpu.VMEM)
unread = pl.BlockSpec(memory_space=pl.ANY)


def limit(mebibytes):
    return pltpu.CompilerParams(vmem_limit_bytes=mebibytes * 1024 * 1024)


def ring(size, step):
    return [(i, (i + 2 * step) % size) for i in range(size)]


def swap(size):
    return [(i, i ^ 1) for i in range(size)]


def far_first(depth):
    return sorted(range(1, depth), key=lambda d: -min(d, depth - d))


def wide(value):
    return value.astype(jnp.float32)


def narrow(value):
    return value.astype(jnp.bfloat16)


def pack_heads(z, queries, key_rows, value_rows, expert_ids, gate_weights, depth):
    rows = queries.shape[0]
    columns = queries.shape[1] // depth
    per_group = queries.shape[1] // key_rows.shape[1] * HD
    top, tokens = expert_ids.shape
    lines = tokens // 4

    def kernel(z_ref, query_ref, key_ref, value_ref, id_ref, gate_ref, *out_refs):
        gates = gate_ref[...]
        high = wide(narrow(gates))
        blank = jnp.zeros((HD // 2 - 3 * top, tokens), jnp.float32)
        meta = jnp.concatenate([wide(id_ref[...]), high, gates - high, blank], axis=0).T
        meta = jnp.concatenate([meta[g * lines : (g + 1) * lines] for g in range(4)], axis=1)
        for d, out_ref in enumerate(out_refs[:depth]):
            start = (z_ref[0] + d) % depth * columns
            group = pl.ds(pl.multiple_of(start // per_group * HD, HD), HD)
            out_ref[:rows, :columns] = query_ref[:, pl.ds(pl.multiple_of(start, HD), columns)]
            out_ref[:rows, columns : columns + HD] = key_ref[:, group]
            out_ref[:rows, columns + HD :] = value_ref[:, group]
            out_ref[rows:, :columns] = jnp.zeros((lines, columns), jnp.bfloat16)
            out_ref[rows:, columns:] = narrow(meta)
        out_refs[depth][...] = out_refs[0][:, columns:]

    return pl.pallas_call(
        kernel,
        out_shape=[jax.ShapeDtypeStruct((rows + lines, columns + 2 * HD), queries.dtype)] * depth
        + [jax.ShapeDtypeStruct((rows + lines, 2 * HD), queries.dtype)],
        in_specs=[smem] + [vmem] * 5,
        out_specs=[vmem] * (depth + 1),
        compiler_params=limit(56),
        name="pack_heads",
    )(z, queries, key_rows, value_rows, expert_ids, gate_weights)


def pack_weight(z, out_weight, depth, before):
    rows = out_weight.shape[0]
    columns = out_weight.shape[1] // depth

    def kernel(z_ref, weight_ref, *refs):
        for d, out_ref in enumerate(refs[len(before) :]):
            start = pl.multiple_of((z_ref[0] + d) % depth * columns, HD)
            out_ref[...] = weight_ref[:, pl.ds(start, columns)]

    return pl.pallas_call(
        kernel,
        out_shape=[jax.ShapeDtypeStruct((rows, columns), out_weight.dtype)] * depth,
        in_specs=[smem, vmem] + [unread] * len(before),
        out_specs=[vmem] * depth,
        compiler_params=limit(16),
        name="pack_weight",
    )(z, out_weight, *before)


def collect_meta(near, across, rows):
    lines = across[0].shape[0] - rows
    parts = [part for pair in zip(near, across) for part in pair]

    def kernel(*refs):
        for i, ref in enumerate(refs[:-1]):
            refs[-1][i * lines : (i + 1) * lines, :] = ref[rows:, -2 * HD :]

    return pl.pallas_call(
        kernel,
        out_shape=jax.ShapeDtypeStruct((len(parts) * lines, 2 * HD), jnp.bfloat16),
        in_specs=[vmem] * len(parts),
        out_specs=vmem,
        compiler_params=limit(16),
        name="collect_meta",
    )(*parts)


def attend(core, starts, key_pos, messages, across, rows, columns):
    depth = len(messages)
    heads = columns // HD
    length = 2 * depth * rows
    half = rows // 2

    def kernel(core_ref, starts_ref, key_pos_ref, *refs):
        message_refs, across_refs = refs[:depth], refs[depth : 2 * depth]
        out_refs, (query, keyed) = refs[-2 - depth : -2], refs[-2:]
        for d in range(depth):
            for h in range(heads):
                query[d, h * rows : (h + 1) * rows, :] = message_refs[d][:rows, h * HD : (h + 1) * HD]
            keyed[2 * d * rows : (2 * d + 1) * rows, :] = message_refs[d][:rows, columns:]
            keyed[(2 * d + 1) * rows : (2 * d + 2) * rows, :] = across_refs[d][:rows, :]
        mine = core_ref[0] == 0

        for d in range(depth):
            scores = lax.dot_general(
                query[d], keyed[:, :HD], (((1,), (1,)), ((), ())), preferred_element_type=jnp.float32
            )
            offset = lax.broadcasted_iota(jnp.int32, (heads * rows, 1), 0) % rows
            allowed = key_pos_ref[...] <= starts_ref[d] + offset
            scores = jnp.where(allowed, scores, neg_large)
            largest = jnp.max(scores, axis=-1, keepdims=True)
            exps = jnp.exp((scores - largest) * (HD**-0.5))
            total = jnp.sum(exps, axis=-1, keepdims=True)
            summed = jnp.dot(narrow(exps), keyed[:, HD:], preferred_element_type=jnp.float32)
            context = narrow(summed / total)
            for h in range(heads):
                low, high = context[h * rows : h * rows + half], context[h * rows + half : (h + 1) * rows]
                out_refs[d][:half, h * HD : (h + 1) * HD] = jnp.where(mine, low, high)
                out_refs[d][half:, h * HD : (h + 1) * HD] = jnp.where(mine, high, low)

    work = depth * rows * columns * length
    return pl.pallas_call(
        kernel,
        out_shape=[jax.ShapeDtypeStruct((rows, columns), jnp.bfloat16)] * depth,
        in_specs=[smem, smem, vmem] + [vmem] * (2 * depth),
        out_specs=[vmem] * depth,
        scratch_shapes=[
            pltpu.VMEM((depth, heads * rows, HD), jnp.bfloat16),
            pltpu.VMEM((length, 2 * HD), jnp.bfloat16),
        ],
        compiler_params=limit(24),
        cost_estimate=pl.CostEstimate(flops=160 * work, bytes_accessed=depth * rows * columns * 8, transcendentals=work // HD),
        name="attend",
    )(core, starts, key_pos, *messages, *across)


def project(place, context, weights, before):
    depth, blocks = len(context), len(weights)
    rows, columns = context[0].shape[0] // 2, context[0].shape[1]
    features = weights[0].shape[0]
    shape = (depth, rows, blocks * features)
    if features % HD:
        weight = jnp.stack(weights)[jnp.argsort(place)]
        left = jnp.stack(context).reshape(depth, 2, rows, columns)
        result = jnp.einsum("dcrk,bfk->cdrbf", left, weight, preferred_element_type=jnp.float32)
        result = narrow(result.reshape((2,) + shape))
        return result[0], result[1]

    def kernel(place_ref, *refs):
        context_refs, weight_refs, out_refs = refs[:depth], refs[depth : depth + blocks], refs[-3:-1]
        left_ref = refs[-1]
        for d in range(depth):
            left_ref[2 * d * rows : 2 * (d + 1) * rows, :] = context_refs[d][...]
        left = left_ref[...]
        for i in range(blocks):
            part = narrow(
                lax.dot_general(
                    left, weight_refs[i][...], (((1,), (1,)), ((), ())), preferred_element_type=jnp.float32
                )
            ).reshape(depth, 2, rows, features)
            there = pl.ds(pl.multiple_of(place_ref[i] * features, HD), features)
            for core in range(2):
                out_refs[core][:, :, there] = part[:, core]

    return pl.pallas_call(
        kernel,
        out_shape=[jax.ShapeDtypeStruct(shape, jnp.bfloat16)] * 2,
        in_specs=[smem] + [vmem] * (depth + blocks) + [unread] * len(before),
        out_specs=[vmem, vmem],
        scratch_shapes=[pltpu.VMEM((2 * depth * rows, columns), jnp.bfloat16)],
        compiler_params=limit(20),
        cost_estimate=pl.CostEstimate(
            flops=4 * depth * rows * columns * blocks * features,
            bytes_accessed=2 * blocks * features * columns + 4 * depth * rows * (columns + 2 * blocks * features),
            transcendentals=0,
        ),
        name="project",
    )(place, *context, *weights, *before)


def add_up(parts):
    def kernel(*refs):
        total = wide(refs[0][...])
        for ref in refs[1 : len(parts)]:
            total = total + wide(ref[...])
        refs[-2][...] = total
        refs[-1][...] = narrow(total)

    return pl.pallas_call(
        kernel,
        out_shape=[
            jax.ShapeDtypeStruct(parts[0].shape, jnp.float32),
            jax.ShapeDtypeStruct(parts[0].shape, jnp.bfloat16),
        ],
        in_specs=[vmem] * len(parts),
        out_specs=[vmem, vmem],
        compiler_params=limit(32),
        name="add_up",
    )(*parts)


def attention_block(stream, queries, key_rows, value_rows, out_weight, expert_ids, gate_weights, local_experts):
    size = lax.axis_size("seq")
    depth = size // 2
    z, y = lax.axis_index("seq") // 2, lax.axis_index("seq") % 2
    core = lax.axis_index("exp").astype(jnp.int32).reshape(1)
    rows = queries.shape[0]
    columns = queries.shape[1] // depth
    steps = far_first(depth)
    here = z.astype(jnp.int32).reshape(1)

    *message, keyed = pack_heads(here, queries, key_rows, value_rows, expert_ids.T, gate_weights.T, depth)
    for d in steps:
        message[d] = lax.ppermute(message[d], "seq", ring(size, d))
    across = {}
    for d in [0] + steps:
        across[d] = lax.ppermute(message[d][:, columns:] if d else keyed, "seq", swap(size))
    across = [across[d] for d in range(depth)]
    weight = list(pack_weight(here, out_weight, depth, [message[steps[0]]]))
    weight_across = {0: lax.ppermute(weight[0], "seq", swap(size))}
    for d in steps[::-1]:
        weight[d] = lax.ppermute(weight[d], "seq", ring(size, d))
        weight_across[d] = lax.ppermute(weight[d], "seq", swap(size))
    first = (lax.axis_index("seq") * 2 + lax.axis_index("exp")) * local_experts
    meta = collect_meta(message, across, rows)
    meta = [meta, lax.ppermute(meta, "exp", swap(2))]
    route = routing(first, meta, depth, *expert_ids.shape, local_experts, [weight_across[0]])

    behind = (z - jnp.arange(depth, dtype=jnp.int32)) % depth
    block = (behind[:, None] * 2 + jnp.stack([y, 1 - y])[None, :]).astype(jnp.int32)
    key_pos = (block.reshape(-1, 1) * rows + jnp.arange(rows, dtype=jnp.int32)).reshape(1, -1)
    context = attend(core, block[:, 0] * rows, key_pos, message, across, rows, columns)
    kept, given = project(
        block.reshape(-1), context, [part for d in range(depth) for part in (weight[d], weight_across[d])], route[1:]
    )
    chip = wide(kept) + wide(lax.ppermute(given, "exp", swap(2)))
    parts = [stream, chip[0]]
    for d in steps:
        parts.append(lax.ppermute(narrow(chip[d]), "seq", ring(size, -d)))
    return *add_up(parts), route


def routing(first, meta, subs, rows, top, local_experts, before):
    lines = rows // 4
    tokens = 4 * rows
    slots = 4 * CAP
    lanes = 128
    contract = lambda a, b, i, j: lax.dot_general(a, b, (((i,), (j,)), ((), ())), preferred_element_type=jnp.float32)
    iota = lambda shape, axis: lax.broadcasted_iota(jnp.int32, shape, axis)

    def kernel(first_ref, mine_ref, other_ref, *refs):
        select_ref, spread_ref, gate_ref = refs[len(before) :]
        token, other = iota((tokens, tokens), 0), iota((tokens, tokens), 1)
        earlier = narrow(wide((other < token) & (other // rows == token // rows)))
        same = narrow(wide(token == other))
        lane = iota((tokens, lanes), 1)
        owner = narrow(wide(iota((lanes, local_experts * slots), 1) // slots == iota((lanes, local_experts * slots), 0)))
        slot = iota((local_experts * slots, tokens), 0)
        fits = slot % slots // CAP == iota((local_experts * slots, tokens), 1) // rows
        for s in range(subs):
            packed = []
            for ref in (mine_ref, other_ref):
                for y in range(2):
                    block = wide(ref[(2 * s + y) * lines : (2 * s + y + 1) * lines, :])
                    packed += [block[:, g * HD // 2 : g * HD // 2 + 3 * top] for g in range(4)]
            packed = jnp.concatenate(packed, axis=0)
            hit = jnp.zeros((tokens, lanes), jnp.float32)
            high, low = hit, hit
            for j in range(local_experts):
                match = packed[:, :top] == wide(first_ref[0] + j)
                column = lambda kind: jnp.sum(jnp.where(match, kind, 0.0), axis=1, keepdims=True)
                here = lane == j
                hit = jnp.where(here, column(1.0), hit)
                high = jnp.where(here, column(packed[:, top : 2 * top]), high)
                low = jnp.where(here, column(packed[:, 2 * top :]), low)
            place = contract(earlier, narrow(hit), 1, 0)
            by_slot = lambda value: contract(owner, narrow(value), 0, 1)
            chosen = (by_slot(hit) > 0.5) & (jnp.abs(by_slot(place) - wide(slot % CAP)) < 0.5) & fits
            gates = jnp.sum(jnp.where(chosen, by_slot(high) + by_slot(low), 0.0), axis=1, keepdims=True)
            chosen = narrow(wide(chosen))
            spread_ref[s] = narrow(contract(same, chosen, 1, 1))
            for j in range(local_experts):
                select_ref[j, s] = chosen[j * slots : (j + 1) * slots]
                gate_ref[j, s * slots : (s + 1) * slots, :] = gates[j * slots : (j + 1) * slots]

    return pl.pallas_call(
        kernel,
        out_shape=[
            jax.ShapeDtypeStruct((local_experts, subs, slots, tokens), jnp.bfloat16),
            jax.ShapeDtypeStruct((subs, tokens, local_experts * slots), jnp.bfloat16),
            jax.ShapeDtypeStruct((local_experts, subs * slots, 1), jnp.float32),
        ],
        in_specs=[smem, vmem, vmem] + [unread] * len(before),
        out_specs=[vmem] * 3,
        compiler_params=limit(32),
        name="routing",
    )(first.astype(jnp.int32).reshape(1), *meta, *before)


def run_experts(mine, other, select, spread, row_gate, norm_gain, expert_in, expert_out):
    subs = len(mine)
    tokens, width = mine[0].shape
    local_experts, hidden, _ = expert_out.shape
    slots = select.shape[2]
    held = min(local_experts, 2)
    batch = min(subs, 4)
    room = 8 * subs * tokens * width + 6 * held * hidden * width + 4 * local_experts * subs * slots * width

    def kernel(select_ref, spread_ref, gate_ref, gain_ref, wi_ref, wo_ref, *refs):
        mine_refs, other_refs = refs[:subs], refs[subs : 2 * subs]
        kept_refs, given_refs = refs[2 * subs : 3 * subs], refs[3 * subs : 4 * subs]
        first, second, xg, res, sem = refs[4 * subs :]

        def copy(e, part):
            if part < 2:
                source, target = wi_ref.at[e, :, part * hidden : (part + 1) * hidden], first.at[e % held, part]
            else:
                source, target = wo_ref.at[e], second.at[e % held]
            return pltpu.make_async_copy(source, target, sem.at[e % held, part])

        def arrive(e, part):
            copy(e, part).wait()
            if e + 1 < local_experts:
                copy(e + 1, part).start()

        for part in range(3):
            copy(0, part).start()
        for s in range(subs):
            choose = select_ref[:, s].reshape(local_experts * slots, 2 * tokens)
            picked = jnp.dot(
                choose[:, :tokens], mine_refs[s][...], preferred_element_type=jnp.float32
            ) + jnp.dot(choose[:, tokens:], other_refs[s][...], preferred_element_type=jnp.float32)
            scale = lax.rsqrt(jnp.sum(picked * picked, axis=1, keepdims=True) * (1.0 / width) + 1e-06)
            rows = narrow(picked * scale * gain_ref[...])
            for e in range(local_experts):
                xg[e, s * slots : (s + 1) * slots, :] = rows[e * slots : (e + 1) * slots]
        for e in range(local_experts):
            for at in range(0, subs, batch):
                span = slice(at * slots, (at + batch) * slots)
                rows = xg[e, span, :]
                if at == 0:
                    arrive(e, 0)
                gate = jnp.dot(rows, first[e % held, 0], preferred_element_type=jnp.float32)
                if at == 0:
                    arrive(e, 1)
                up = jnp.dot(rows, first[e % held, 1], preferred_element_type=jnp.float32)
                act = narrow(gate / (1.0 + jnp.exp(-gate)) * up)
                if at == 0:
                    arrive(e, 2)
                part = jnp.dot(act, second[e % held], preferred_element_type=jnp.float32)
                scaled = narrow(part * gate_ref[e, span, :])
                for s in range(batch):
                    res[at + s, e * slots : (e + 1) * slots, :] = scaled[s * slots : (s + 1) * slots]
        for s in range(subs):
            both = narrow(jnp.dot(spread_ref[s], res[s], preferred_element_type=jnp.float32))
            kept_refs[s][...] = both[:tokens]
            given_refs[s][...] = both[tokens:]

    flops = local_experts * subs * slots * width * hidden * 6
    moved = (expert_in.size + expert_out.size + 8 * subs * tokens * width) * 2
    outs = pl.pallas_call(
        kernel,
        out_shape=[jax.ShapeDtypeStruct((tokens, width), jnp.bfloat16)] * (2 * subs),
        in_specs=[vmem] * 4 + [unread] * 2 + [vmem] * (2 * subs),
        out_specs=[vmem] * (2 * subs),
        scratch_shapes=[
            pltpu.VMEM((held, 2, width, hidden), jnp.bfloat16),
            pltpu.VMEM((held, hidden, width), jnp.bfloat16),
            pltpu.VMEM((local_experts, subs * slots, width), jnp.bfloat16),
            pltpu.VMEM((subs, local_experts * slots, width), jnp.bfloat16),
            pltpu.SemaphoreType.DMA((held, 3)),
        ],
        compiler_params=limit(room * 9 // 8 // 2**20),
        cost_estimate=pl.CostEstimate(flops=flops, bytes_accessed=moved, transcendentals=0),
        name="experts",
    )(select, spread, row_gate, norm_gain.reshape(1, -1), expert_in, expert_out, *mine, *other)
    return outs[:subs], outs[subs:]


def expert_block(mixed, rounded, route, norm_gain, expert_in, expert_out):
    size = lax.axis_size("seq")
    depth = size // 2
    rows = mixed.shape[0]

    along, mine, other = [rounded], [], []
    for d in range(depth):
        if d + 1 < depth:
            along.append(lax.ppermute(along[d], "seq", ring(size, 1)))
        mine.append(jnp.concatenate([along[d], lax.ppermute(along[d], "seq", swap(size))]))
        other.append(lax.ppermute(mine[d], "exp", swap(2)))
    kept, given = run_experts(mine, other, *route, norm_gain, expert_in, expert_out)

    total = mixed
    for d in far_first(depth) + [0]:
        pair = wide(kept[d]) + wide(lax.ppermute(given[d], "exp", swap(2)))
        there = lax.ppermute(narrow(pair[rows:]), "seq", swap(size))
        chip = pair[:rows] + wide(there)
        if d:
            chip = wide(lax.ppermute(narrow(chip), "seq", ring(size, -d)))
        total = total + chip
    return narrow(total)


def on_device(
    stream,
    queries,
    key_rows,
    value_rows,
    out_weight,
    norm_gain,
    expert_ids,
    gate_weights,
    expert_in,
    expert_out,
):
    mixed, rounded, route = attention_block(
        stream, queries, key_rows, value_rows, out_weight, expert_ids, gate_weights, expert_in.shape[0]
    )
    return expert_block(mixed, rounded, route, norm_gain, expert_in, expert_out)


def solution(mesh):
    in_specs = (
        P(("groups", "seq", "exp"), None),
        P(("groups", "seq"), "exp"),
        P(("groups", "seq"), "exp"),
        P(("groups", "seq"), "exp"),
        P("seq", "exp"),
        P(),
        P(("groups", "seq", "exp"), None),
        P(("groups", "seq", "exp"), None),
        P(("seq", "exp"), None, None),
        P(("seq", "exp"), None, None),
    )
    out_specs = P(("groups", "seq", "exp"), None)
    return jax.shard_map(
        on_device, mesh=mesh, in_specs=in_specs, out_specs=out_specs, check_vma=False
    )
```

```python
import jax
import jax.numpy as jnp
from jax import lax
from jax.experimental import pallas as pl
from jax.experimental.pallas import tpu as pltpu
from jax.sharding import PartitionSpec as P

HD = 128
CAP = 12
AHEAD = 3

neg_large = -1e30
smem = pl.BlockSpec(memory_space=pltpu.SMEM)
vmem = pl.BlockSpec(memory_space=pltpu.VMEM)
unread = pl.BlockSpec(memory_space=pl.ANY)


def limit(mebibytes):
    return pltpu.CompilerParams(vmem_limit_bytes=mebibytes * 1024 * 1024)


def ring(size, step):
    return [(i, (i + 2 * step) % size) for i in range(size)]


def swap(size):
    return [(i, i ^ 1) for i in range(size)]


def far_first(depth):
    return sorted(range(1, depth), key=lambda d: -min(d, depth - d))


def wide(value):
    return value.astype(jnp.float32)


def narrow(value):
    return value.astype(jnp.bfloat16)


def pack_heads(z, queries, key_rows, value_rows, expert_ids, gate_weights, depth):
    rows = queries.shape[0]
    columns = queries.shape[1] // depth
    per_group = queries.shape[1] // key_rows.shape[1] * HD
    top, tokens = expert_ids.shape
    lines = tokens // 4

    def kernel(z_ref, query_ref, key_ref, value_ref, id_ref, gate_ref, *out_refs):
        gates = gate_ref[...]
        high = wide(narrow(gates))
        blank = jnp.zeros((HD // 2 - 3 * top, tokens), jnp.float32)
        meta = jnp.concatenate([wide(id_ref[...]), high, gates - high, blank], axis=0).T
        meta = jnp.concatenate([meta[g * lines : (g + 1) * lines] for g in range(4)], axis=1)
        for d, out_ref in enumerate(out_refs[:depth]):
            start = (z_ref[0] + d) % depth * columns
            group = pl.ds(pl.multiple_of(start // per_group * HD, HD), HD)
            out_ref[:rows, :columns] = query_ref[:, pl.ds(pl.multiple_of(start, HD), columns)]
            out_ref[:rows, columns : columns + HD] = key_ref[:, group]
            out_ref[:rows, columns + HD :] = value_ref[:, group]
            out_ref[rows:, :columns] = jnp.zeros((lines, columns), jnp.bfloat16)
            out_ref[rows:, columns:] = narrow(meta)
        out_refs[depth][...] = out_refs[0][:, columns:]

    return pl.pallas_call(
        kernel,
        out_shape=[jax.ShapeDtypeStruct((rows + lines, columns + 2 * HD), queries.dtype)] * depth
        + [jax.ShapeDtypeStruct((rows + lines, 2 * HD), queries.dtype)],
        in_specs=[smem] + [vmem] * 5,
        out_specs=[vmem] * (depth + 1),
        compiler_params=limit(56),
        name="pack_heads",
    )(z, queries, key_rows, value_rows, expert_ids, gate_weights)


def pack_weight(z, out_weight, depth, before):
    rows = out_weight.shape[0]
    columns = out_weight.shape[1] // depth

    def kernel(z_ref, weight_ref, *refs):
        for d, out_ref in enumerate(refs[len(before) :]):
            start = pl.multiple_of((z_ref[0] + d) % depth * columns, HD)
            out_ref[...] = weight_ref[:, pl.ds(start, columns)]

    return pl.pallas_call(
        kernel,
        out_shape=[jax.ShapeDtypeStruct((rows, columns), out_weight.dtype)] * depth,
        in_specs=[smem, vmem] + [unread] * len(before),
        out_specs=[vmem] * depth,
        compiler_params=limit(16),
        name="pack_weight",
    )(z, out_weight, *before)


def collect_meta(near, across, rows):
    lines = across[0].shape[0] - rows
    parts = [part for pair in zip(near, across) for part in pair]

    def kernel(*refs):
        for i, ref in enumerate(refs[:-1]):
            refs[-1][i * lines : (i + 1) * lines, :] = ref[rows:, -2 * HD :]

    return pl.pallas_call(
        kernel,
        out_shape=jax.ShapeDtypeStruct((len(parts) * lines, 2 * HD), jnp.bfloat16),
        in_specs=[vmem] * len(parts),
        out_specs=vmem,
        compiler_params=limit(16),
        name="collect_meta",
    )(*parts)


def attend(core, starts, key_pos, messages, across, rows, columns):
    depth = len(messages)
    heads = columns // HD
    length = 2 * depth * rows
    half = rows // 2

    def kernel(core_ref, starts_ref, key_pos_ref, *refs):
        message_refs, across_refs = refs[:depth], refs[depth : 2 * depth]
        out_refs, (query, keyed) = refs[-2 - depth : -2], refs[-2:]
        for d in range(depth):
            for h in range(heads):
                query[d, h * rows : (h + 1) * rows, :] = message_refs[d][:rows, h * HD : (h + 1) * HD]
            keyed[2 * d * rows : (2 * d + 1) * rows, :] = message_refs[d][:rows, columns:]
            keyed[(2 * d + 1) * rows : (2 * d + 2) * rows, :] = across_refs[d][:rows, :]
        mine = core_ref[0] == 0

        for d in range(depth):
            scores = lax.dot_general(
                query[d], keyed[:, :HD], (((1,), (1,)), ((), ())), preferred_element_type=jnp.float32
            )
            offset = lax.broadcasted_iota(jnp.int32, (heads * rows, 1), 0) % rows
            allowed = key_pos_ref[...] <= starts_ref[d] + offset
            scores = jnp.where(allowed, scores, neg_large)
            largest = jnp.max(scores, axis=-1, keepdims=True)
            exps = jnp.exp((scores - largest) * (HD**-0.5))
            total = jnp.sum(exps, axis=-1, keepdims=True)
            summed = jnp.dot(narrow(exps), keyed[:, HD:], preferred_element_type=jnp.float32)
            context = narrow(summed / total)
            for h in range(heads):
                low, high = context[h * rows : h * rows + half], context[h * rows + half : (h + 1) * rows]
                out_refs[d][:half, h * HD : (h + 1) * HD] = jnp.where(mine, low, high)
                out_refs[d][half:, h * HD : (h + 1) * HD] = jnp.where(mine, high, low)

    work = depth * rows * columns * length
    return pl.pallas_call(
        kernel,
        out_shape=[jax.ShapeDtypeStruct((rows, columns), jnp.bfloat16)] * depth,
        in_specs=[smem, smem, vmem] + [vmem] * (2 * depth),
        out_specs=[vmem] * depth,
        scratch_shapes=[
            pltpu.VMEM((depth, heads * rows, HD), jnp.bfloat16),
            pltpu.VMEM((length, 2 * HD), jnp.bfloat16),
        ],
        compiler_params=limit(24),
        cost_estimate=pl.CostEstimate(flops=160 * work, bytes_accessed=depth * rows * columns * 8, transcendentals=work // HD),
        name="attend",
    )(core, starts, key_pos, *messages, *across)


def project(place, context, weights, before):
    depth, blocks = len(context), len(weights)
    rows, columns = context[0].shape[0] // 2, context[0].shape[1]
    features = weights[0].shape[0]
    shape = (depth, rows, blocks * features)
    if features % HD:
        weight = jnp.stack(weights)[jnp.argsort(place)]
        left = jnp.stack(context).reshape(depth, 2, rows, columns)
        result = jnp.einsum("dcrk,bfk->cdrbf", left, weight, preferred_element_type=jnp.float32)
        result = narrow(result.reshape((2,) + shape))
        return result[0], result[1]

    def kernel(place_ref, *refs):
        context_refs, weight_refs, out_refs = refs[:depth], refs[depth : depth + blocks], refs[-3:-1]
        left_ref = refs[-1]
        for d in range(depth):
            left_ref[2 * d * rows : 2 * (d + 1) * rows, :] = context_refs[d][...]
        left = left_ref[...]
        for i in range(blocks):
            part = narrow(
                lax.dot_general(
                    left, weight_refs[i][...], (((1,), (1,)), ((), ())), preferred_element_type=jnp.float32
                )
            ).reshape(depth, 2, rows, features)
            there = pl.ds(pl.multiple_of(place_ref[i] * features, HD), features)
            for core in range(2):
                out_refs[core][:, :, there] = part[:, core]

    return pl.pallas_call(
        kernel,
        out_shape=[jax.ShapeDtypeStruct(shape, jnp.bfloat16)] * 2,
        in_specs=[smem] + [vmem] * (depth + blocks) + [unread] * len(before),
        out_specs=[vmem, vmem],
        scratch_shapes=[pltpu.VMEM((2 * depth * rows, columns), jnp.bfloat16)],
        compiler_params=limit(20),
        cost_estimate=pl.CostEstimate(
            flops=4 * depth * rows * columns * blocks * features,
            bytes_accessed=2 * blocks * features * columns + 4 * depth * rows * (columns + 2 * blocks * features),
            transcendentals=0,
        ),
        name="project",
    )(place, *context, *weights, *before)


def add_up(parts):
    def kernel(*refs):
        total = wide(refs[0][...])
        for ref in refs[1 : len(parts)]:
            total = total + wide(ref[...])
        refs[-2][...] = total
        refs[-1][...] = narrow(total)

    return pl.pallas_call(
        kernel,
        out_shape=[
            jax.ShapeDtypeStruct(parts[0].shape, jnp.float32),
            jax.ShapeDtypeStruct(parts[0].shape, jnp.bfloat16),
        ],
        in_specs=[vmem] * len(parts),
        out_specs=[vmem, vmem],
        compiler_params=limit(32),
        name="add_up",
    )(*parts)


def attention_block(stream, queries, key_rows, value_rows, out_weight, expert_ids, gate_weights, local_experts):
    size = lax.axis_size("seq")
    depth = size // 2
    z, y = lax.axis_index("seq") // 2, lax.axis_index("seq") % 2
    core = lax.axis_index("exp").astype(jnp.int32).reshape(1)
    rows = queries.shape[0]
    columns = queries.shape[1] // depth
    steps = far_first(depth)
    here = z.astype(jnp.int32).reshape(1)

    *message, keyed = pack_heads(here, queries, key_rows, value_rows, expert_ids.T, gate_weights.T, depth)
    for d in steps:
        message[d] = lax.ppermute(message[d], "seq", ring(size, d))
    across = {}
    for d in [0] + steps:
        across[d] = lax.ppermute(message[d][:, columns:] if d else keyed, "seq", swap(size))
    across = [across[d] for d in range(depth)]
    weight = list(pack_weight(here, out_weight, depth, [message[steps[0]]]))
    weight_across = {0: lax.ppermute(weight[0], "seq", swap(size))}
    for d in steps[::-1]:
        weight[d] = lax.ppermute(weight[d], "seq", ring(size, d))
        weight_across[d] = lax.ppermute(weight[d], "seq", swap(size))
    first = (lax.axis_index("seq") * 2 + lax.axis_index("exp")) * local_experts
    meta = collect_meta(message, across, rows)
    meta = [meta, lax.ppermute(meta, "exp", swap(2))]
    route = routing(first, meta, depth, *expert_ids.shape, local_experts, [weight_across[0]])

    behind = (z - jnp.arange(depth, dtype=jnp.int32)) % depth
    block = (behind[:, None] * 2 + jnp.stack([y, 1 - y])[None, :]).astype(jnp.int32)
    key_pos = (block.reshape(-1, 1) * rows + jnp.arange(rows, dtype=jnp.int32)).reshape(1, -1)
    context = attend(core, block[:, 0] * rows, key_pos, message, across, rows, columns)
    kept, given = project(
        block.reshape(-1), context, [part for d in range(depth) for part in (weight[d], weight_across[d])], route[1:]
    )
    chip = wide(kept) + wide(lax.ppermute(given, "exp", swap(2)))
    parts = [stream, chip[0]]
    for d in steps:
        parts.append(lax.ppermute(narrow(chip[d]), "seq", ring(size, -d)))
    return *add_up(parts), route


def routing(first, meta, subs, rows, top, local_experts, before):
    lines = rows // 4
    tokens = 4 * rows
    slots = 4 * CAP
    lanes = 128
    contract = lambda a, b, i, j: lax.dot_general(a, b, (((i,), (j,)), ((), ())), preferred_element_type=jnp.float32)
    iota = lambda shape, axis: lax.broadcasted_iota(jnp.int32, shape, axis)

    def kernel(first_ref, mine_ref, other_ref, *refs):
        select_ref, spread_ref, gate_ref = refs[len(before) :]
        token, other = iota((tokens, tokens), 0), iota((tokens, tokens), 1)
        earlier = narrow(wide((other < token) & (other // rows == token // rows)))
        same = narrow(wide(token == other))
        lane = iota((tokens, lanes), 1)
        owner = narrow(wide(iota((lanes, local_experts * slots), 1) // slots == iota((lanes, local_experts * slots), 0)))
        slot = iota((local_experts * slots, tokens), 0)
        fits = slot % slots // CAP == iota((local_experts * slots, tokens), 1) // rows
        for s in range(subs):
            packed = []
            for ref in (mine_ref, other_ref):
                for y in range(2):
                    block = wide(ref[(2 * s + y) * lines : (2 * s + y + 1) * lines, :])
                    packed += [block[:, g * HD // 2 : g * HD // 2 + 3 * top] for g in range(4)]
            packed = jnp.concatenate(packed, axis=0)
            hit = jnp.zeros((tokens, lanes), jnp.float32)
            high, low = hit, hit
            for j in range(local_experts):
                match = packed[:, :top] == wide(first_ref[0] + j)
                column = lambda kind: jnp.sum(jnp.where(match, kind, 0.0), axis=1, keepdims=True)
                here = lane == j
                hit = jnp.where(here, column(1.0), hit)
                high = jnp.where(here, column(packed[:, top : 2 * top]), high)
                low = jnp.where(here, column(packed[:, 2 * top :]), low)
            place = contract(earlier, narrow(hit), 1, 0)
            by_slot = lambda value: contract(owner, narrow(value), 0, 1)
            chosen = (by_slot(hit) > 0.5) & (jnp.abs(by_slot(place) - wide(slot % CAP)) < 0.5) & fits
            gates = jnp.sum(jnp.where(chosen, by_slot(high) + by_slot(low), 0.0), axis=1, keepdims=True)
            chosen = narrow(wide(chosen))
            spread_ref[s] = narrow(contract(same, chosen, 1, 1))
            for j in range(local_experts):
                select_ref[j, s] = chosen[j * slots : (j + 1) * slots]
                gate_ref[j, s * slots : (s + 1) * slots, :] = gates[j * slots : (j + 1) * slots]

    return pl.pallas_call(
        kernel,
        out_shape=[
            jax.ShapeDtypeStruct((local_experts, subs, slots, tokens), jnp.bfloat16),
            jax.ShapeDtypeStruct((subs, tokens, local_experts * slots), jnp.bfloat16),
            jax.ShapeDtypeStruct((local_experts, subs * slots, 1), jnp.float32),
        ],
        in_specs=[smem, vmem, vmem] + [unread] * len(before),
        out_specs=[vmem] * 3,
        compiler_params=limit(32),
        name="routing",
    )(first.astype(jnp.int32).reshape(1), *meta, *before)


def run_experts(mine, other, select, spread, row_gate, norm_gain, expert_in, expert_out):
    subs = len(mine)
    tokens, width = mine[0].shape
    local_experts, hidden, _ = expert_out.shape
    slots = select.shape[2]
    held = min(local_experts, 2)
    batch = min(subs, 4)
    room = 8 * subs * tokens * width + 6 * held * hidden * width + 4 * local_experts * subs * slots * width

    def kernel(select_ref, spread_ref, gate_ref, gain_ref, wi_ref, wo_ref, *refs):
        mine_refs, other_refs = refs[:subs], refs[subs : 2 * subs]
        kept_refs, given_refs = refs[2 * subs : 3 * subs], refs[3 * subs : 4 * subs]
        first, second, x, xg, res, sem = refs[4 * subs :]

        def copy(e, part):
            if part < 2:
                source, target = wi_ref.at[e, :, part * hidden : (part + 1) * hidden], first.at[e % held, part]
            else:
                source, target = wo_ref.at[e], second.at[e % held]
            return pltpu.make_async_copy(source, target, sem.at[e % held, part])

        def arrive(e, part):
            copy(e, part).wait()
            coming = 3 * e + part + AHEAD
            if coming < 3 * local_experts:
                copy(coming // 3, coming % 3).start()

        for part in range(AHEAD):
            copy(0, part).start()
        for s in range(subs):
            choose = select_ref[:, s].reshape(local_experts * slots, 2 * tokens)
            x[s % 2, :tokens, :] = mine_refs[s][...]
            x[s % 2, tokens:, :] = other_refs[s][...]
            picked = jnp.dot(choose, x[s % 2], preferred_element_type=jnp.float32)
            scale = lax.rsqrt(jnp.sum(picked * picked, axis=1, keepdims=True) * (1.0 / width) + 1e-06)
            rows = narrow(picked * scale * gain_ref[...])
            for e in range(local_experts):
                xg[e, s * slots : (s + 1) * slots, :] = rows[e * slots : (e + 1) * slots]
        for e in range(local_experts):
            for at in range(0, subs, batch):
                span = slice(at * slots, (at + batch) * slots)
                rows = xg[e, span, :]
                if at == 0:
                    arrive(e, 0)
                gate = jnp.dot(rows, first[e % held, 0], preferred_element_type=jnp.float32)
                if at == 0:
                    arrive(e, 1)
                up = jnp.dot(rows, first[e % held, 1], preferred_element_type=jnp.float32)
                act = narrow(gate / (1.0 + jnp.exp(-gate)) * up)
                if at == 0:
                    arrive(e, 2)
                part = jnp.dot(act, second[e % held], preferred_element_type=jnp.float32)
                scaled = narrow(part * gate_ref[e, span, :])
                for s in range(batch):
                    res[at + s, e * slots : (e + 1) * slots, :] = scaled[s * slots : (s + 1) * slots]
        for s in range(subs):
            both = narrow(jnp.dot(spread_ref[s], res[s], preferred_element_type=jnp.float32))
            kept_refs[s][...] = both[:tokens]
            given_refs[s][...] = both[tokens:]

    flops = local_experts * subs * slots * width * hidden * 6
    moved = (expert_in.size + expert_out.size + 8 * subs * tokens * width) * 2
    outs = pl.pallas_call(
        kernel,
        out_shape=[jax.ShapeDtypeStruct((tokens, width), jnp.bfloat16)] * (2 * subs),
        in_specs=[vmem] * 4 + [unread] * 2 + [vmem] * (2 * subs),
        out_specs=[vmem] * (2 * subs),
        scratch_shapes=[
            pltpu.VMEM((held, 2, width, hidden), jnp.bfloat16),
            pltpu.VMEM((held, hidden, width), jnp.bfloat16),
            pltpu.VMEM((2, 2 * tokens, width), jnp.bfloat16),
            pltpu.VMEM((local_experts, subs * slots, width), jnp.bfloat16),
            pltpu.VMEM((subs, local_experts * slots, width), jnp.bfloat16),
            pltpu.SemaphoreType.DMA((held, 3)),
        ],
        compiler_params=limit(room * 19 // 16 // 2**20),
        cost_estimate=pl.CostEstimate(flops=flops, bytes_accessed=moved, transcendentals=0),
        name="experts",
    )(select, spread, row_gate, norm_gain.reshape(1, -1), expert_in, expert_out, *mine, *other)
    return outs[:subs], outs[subs:]


def expert_block(mixed, rounded, route, norm_gain, expert_in, expert_out):
    size = lax.axis_size("seq")
    depth = size // 2
    rows = mixed.shape[0]

    along, mine, other = [rounded], [], []
    for d in range(depth):
        if d + 1 < depth:
            along.append(lax.ppermute(along[d], "seq", ring(size, 1)))
        if 0 < d == depth - 1:
            across = lax.ppermute(first, "seq", ring(size, d))
        else:
            across = lax.ppermute(along[d], "seq", swap(size))
        if d == 0:
            first = across
        mine.append(jnp.concatenate([along[d], across]))
        other.append(lax.ppermute(mine[d], "exp", swap(2)))
    kept, given = run_experts(mine, other, *route, norm_gain, expert_in, expert_out)

    pair = [wide(kept[d]) + wide(lax.ppermute(given[d], "exp", swap(2))) for d in range(depth)]
    last = depth - 1
    there = wide(lax.ppermute(narrow(pair[last]), "seq", ring(size, -last)))
    total = mixed + pair[0][:rows] + there[:rows]
    for d in far_first(depth):
        if d != last:
            chip = pair[d][:rows] + wide(lax.ppermute(narrow(pair[d][rows:]), "seq", swap(size)))
            total = total + wide(lax.ppermute(narrow(chip), "seq", ring(size, -d)))
    across = narrow(pair[0][rows:] + there[rows:])
    return narrow(total + wide(lax.ppermute(across, "seq", swap(size))))


def on_device(
    stream,
    queries,
    key_rows,
    value_rows,
    out_weight,
    norm_gain,
    expert_ids,
    gate_weights,
    expert_in,
    expert_out,
):
    mixed, rounded, route = attention_block(
        stream, queries, key_rows, value_rows, out_weight, expert_ids, gate_weights, expert_in.shape[0]
    )
    return expert_block(mixed, rounded, route, norm_gain, expert_in, expert_out)


def solution(mesh):
    in_specs = (
        P(("groups", "seq", "exp"), None),
        P(("groups", "seq"), "exp"),
        P(("groups", "seq"), "exp"),
        P(("groups", "seq"), "exp"),
        P("seq", "exp"),
        P(),
        P(("groups", "seq", "exp"), None),
        P(("groups", "seq", "exp"), None),
        P(("seq", "exp"), None, None),
        P(("seq", "exp"), None, None),
    )
    out_specs = P(("groups", "seq", "exp"), None)
    return jax.shard_map(
        on_device, mesh=mesh, in_specs=in_specs, out_specs=out_specs, check_vma=False
    )
```

```python
import jax
import jax.numpy as jnp
from jax import lax
from jax.experimental import pallas as pl
from jax.experimental.pallas import tpu as pltpu
from jax.sharding import PartitionSpec as P

HD = 128
CAP = 12
AHEAD = 3

neg_large = -1e30
smem = pl.BlockSpec(memory_space=pltpu.SMEM)
vmem = pl.BlockSpec(memory_space=pltpu.VMEM)
unread = pl.BlockSpec(memory_space=pl.ANY)


def limit(mebibytes):
    return pltpu.CompilerParams(vmem_limit_bytes=mebibytes * 1024 * 1024)


def ring(size, step):
    return [(i, (i + 2 * step) % size) for i in range(size)]


def swap(size):
    return [(i, i ^ 1) for i in range(size)]


def far_first(depth):
    return sorted(range(1, depth), key=lambda d: -min(d, depth - d))


def wide(value):
    return value.astype(jnp.float32)


def narrow(value):
    return value.astype(jnp.bfloat16)


def pack_heads(z, queries, key_rows, value_rows, expert_ids, gate_weights, depth):
    rows = queries.shape[0]
    columns = queries.shape[1] // depth
    per_group = queries.shape[1] // key_rows.shape[1] * HD
    top, tokens = expert_ids.shape
    lines = tokens // 4

    def kernel(z_ref, query_ref, key_ref, value_ref, id_ref, gate_ref, *out_refs):
        gates = gate_ref[...]
        high = wide(narrow(gates))
        blank = jnp.zeros((HD // 2 - 3 * top, tokens), jnp.float32)
        meta = jnp.concatenate([wide(id_ref[...]), high, gates - high, blank], axis=0).T
        meta = jnp.concatenate([meta[g * lines : (g + 1) * lines] for g in range(4)], axis=1)
        for d, out_ref in enumerate(out_refs[:depth]):
            start = (z_ref[0] + d) % depth * columns
            group = pl.ds(pl.multiple_of(start // per_group * HD, HD), HD)
            out_ref[:rows, :columns] = query_ref[:, pl.ds(pl.multiple_of(start, HD), columns)]
            out_ref[:rows, columns : columns + HD] = key_ref[:, group]
            out_ref[:rows, columns + HD :] = value_ref[:, group]
            out_ref[rows:, :columns] = jnp.zeros((lines, columns), jnp.bfloat16)
            out_ref[rows:, columns:] = narrow(meta)
        out_refs[depth][...] = out_refs[0][:, columns:]

    return pl.pallas_call(
        kernel,
        out_shape=[jax.ShapeDtypeStruct((rows + lines, columns + 2 * HD), queries.dtype)] * depth
        + [jax.ShapeDtypeStruct((rows + lines, 2 * HD), queries.dtype)],
        in_specs=[smem] + [vmem] * 5,
        out_specs=[vmem] * (depth + 1),
        compiler_params=limit(56),
        name="pack_heads",
    )(z, queries, key_rows, value_rows, expert_ids, gate_weights)


def pack_weight(z, out_weight, depth, before):
    rows = out_weight.shape[0]
    columns = out_weight.shape[1] // depth

    def kernel(z_ref, weight_ref, *refs):
        for d, out_ref in enumerate(refs[len(before) :]):
            start = pl.multiple_of((z_ref[0] + d) % depth * columns, HD)
            out_ref[...] = weight_ref[:, pl.ds(start, columns)]

    return pl.pallas_call(
        kernel,
        out_shape=[jax.ShapeDtypeStruct((rows, columns), out_weight.dtype)] * depth,
        in_specs=[smem, vmem] + [unread] * len(before),
        out_specs=[vmem] * depth,
        compiler_params=limit(16),
        name="pack_weight",
    )(z, out_weight, *before)


def collect_meta(near, across, rows):
    lines = across[0].shape[0] - rows
    parts = [part for pair in zip(near, across) for part in pair]

    def kernel(*refs):
        for i, ref in enumerate(refs[:-1]):
            refs[-1][i * lines : (i + 1) * lines, :] = ref[rows:, -2 * HD :]

    return pl.pallas_call(
        kernel,
        out_shape=jax.ShapeDtypeStruct((len(parts) * lines, 2 * HD), jnp.bfloat16),
        in_specs=[vmem] * len(parts),
        out_specs=vmem,
        compiler_params=limit(16),
        name="collect_meta",
    )(*parts)


def attend(core, starts, key_pos, messages, across, rows, columns):
    depth = len(messages)
    heads = columns // HD
    length = 2 * depth * rows
    half = rows // 2

    def kernel(core_ref, starts_ref, key_pos_ref, *refs):
        message_refs, across_refs = refs[:depth], refs[depth : 2 * depth]
        out_refs, (query, keyed) = refs[-2 - depth : -2], refs[-2:]
        for d in range(depth):
            for h in range(heads):
                query[d, h * rows : (h + 1) * rows, :] = message_refs[d][:rows, h * HD : (h + 1) * HD]
            keyed[2 * d * rows : (2 * d + 1) * rows, :] = message_refs[d][:rows, columns:]
            keyed[(2 * d + 1) * rows : (2 * d + 2) * rows, :] = across_refs[d][:rows, :]
        mine = core_ref[0] == 0

        for d in range(depth):
            scores = lax.dot_general(
                query[d], keyed[:, :HD], (((1,), (1,)), ((), ())), preferred_element_type=jnp.float32
            )
            offset = lax.broadcasted_iota(jnp.int32, (heads * rows, 1), 0) % rows
            allowed = key_pos_ref[...] <= starts_ref[d] + offset
            scores = jnp.where(allowed, scores, neg_large)
            largest = jnp.max(scores, axis=-1, keepdims=True)
            exps = jnp.exp((scores - largest) * (HD**-0.5))
            total = jnp.sum(exps, axis=-1, keepdims=True)
            summed = jnp.dot(narrow(exps), keyed[:, HD:], preferred_element_type=jnp.float32)
            context = narrow(summed / total)
            for h in range(heads):
                low, high = context[h * rows : h * rows + half], context[h * rows + half : (h + 1) * rows]
                out_refs[d][:half, h * HD : (h + 1) * HD] = jnp.where(mine, low, high)
                out_refs[d][half:, h * HD : (h + 1) * HD] = jnp.where(mine, high, low)

    work = depth * rows * columns * length
    return pl.pallas_call(
        kernel,
        out_shape=[jax.ShapeDtypeStruct((rows, columns), jnp.bfloat16)] * depth,
        in_specs=[smem, smem, vmem] + [vmem] * (2 * depth),
        out_specs=[vmem] * depth,
        scratch_shapes=[
            pltpu.VMEM((depth, heads * rows, HD), jnp.bfloat16),
            pltpu.VMEM((length, 2 * HD), jnp.bfloat16),
        ],
        compiler_params=limit(24),
        cost_estimate=pl.CostEstimate(flops=4 * work, bytes_accessed=depth * rows * columns * 8, transcendentals=work // HD),
        name="attend",
    )(core, starts, key_pos, *messages, *across)


def project(place, context, weights, before):
    depth, blocks = len(context), len(weights)
    rows, columns = context[0].shape[0] // 2, context[0].shape[1]
    features = weights[0].shape[0]
    shape = (rows, blocks * features)
    if features % HD:
        weight = jnp.stack(weights)[jnp.argsort(place)]
        left = jnp.stack(context).reshape(depth, 2, rows, columns)
        result = jnp.einsum("dcrk,bfk->cdrbf", left, weight, preferred_element_type=jnp.float32)
        result = narrow(result.reshape((2, depth) + shape))
        return [[result[core, d] for d in range(depth)] for core in range(2)]

    def kernel(place_ref, *refs):
        context_refs, weight_refs, out_refs = refs[:depth], refs[depth : depth + blocks], refs[-1 - 2 * depth : -1]
        left_ref = refs[-1]
        for d in range(depth):
            left_ref[2 * d * rows : 2 * (d + 1) * rows, :] = context_refs[d][...]
        left = left_ref[...]
        for i in range(blocks):
            part = narrow(
                lax.dot_general(
                    left, weight_refs[i][...], (((1,), (1,)), ((), ())), preferred_element_type=jnp.float32
                )
            ).reshape(depth, 2, rows, features)
            there = pl.ds(pl.multiple_of(place_ref[i] * features, HD), features)
            for d in range(depth):
                for core in range(2):
                    out_refs[core * depth + d][:, there] = part[d, core]

    outs = pl.pallas_call(
        kernel,
        out_shape=[jax.ShapeDtypeStruct(shape, jnp.bfloat16)] * (2 * depth),
        in_specs=[smem] + [vmem] * (depth + blocks) + [unread] * len(before),
        out_specs=[vmem] * (2 * depth),
        scratch_shapes=[pltpu.VMEM((2 * depth * rows, columns), jnp.bfloat16)],
        compiler_params=limit(20),
        cost_estimate=pl.CostEstimate(
            flops=4 * depth * rows * columns * blocks * features,
            bytes_accessed=2 * blocks * features * columns + 4 * depth * rows * (columns + 2 * blocks * features),
            transcendentals=0,
        ),
        name="project",
    )(place, *context, *weights, *before)
    return outs[:depth], outs[depth:]


def add_up(parts):
    def kernel(*refs):
        total = wide(refs[0][...])
        for ref in refs[1 : len(parts)]:
            total = total + wide(ref[...])
        refs[-2][...] = total
        refs[-1][...] = narrow(total)

    return pl.pallas_call(
        kernel,
        out_shape=[
            jax.ShapeDtypeStruct(parts[0].shape, jnp.float32),
            jax.ShapeDtypeStruct(parts[0].shape, jnp.bfloat16),
        ],
        in_specs=[vmem] * len(parts),
        out_specs=[vmem, vmem],
        compiler_params=limit(32),
        name="add_up",
    )(*parts)


def attention_block(stream, queries, key_rows, value_rows, out_weight, expert_ids, gate_weights, local_experts):
    size = lax.axis_size("seq")
    depth = size // 2
    z, y = lax.axis_index("seq") // 2, lax.axis_index("seq") % 2
    core = lax.axis_index("exp").astype(jnp.int32).reshape(1)
    rows = queries.shape[0]
    columns = queries.shape[1] // depth
    steps = far_first(depth)
    here = z.astype(jnp.int32).reshape(1)

    *message, keyed = pack_heads(here, queries, key_rows, value_rows, expert_ids.T, gate_weights.T, depth)
    for d in steps:
        message[d] = lax.ppermute(message[d], "seq", ring(size, d))
    across = {}
    for d in [0] + steps:
        across[d] = lax.ppermute(message[d][:, columns:] if d else keyed, "seq", swap(size))
    across = [across[d] for d in range(depth)]
    weight = list(pack_weight(here, out_weight, depth, [message[steps[0]]]))
    weight_across = {0: lax.ppermute(weight[0], "seq", swap(size))}
    for d in steps[::-1]:
        weight[d] = lax.ppermute(weight[d], "seq", ring(size, d))
        weight_across[d] = lax.ppermute(weight[d], "seq", swap(size))
    first = (lax.axis_index("seq") * 2 + lax.axis_index("exp")) * local_experts
    meta = collect_meta(message, across, rows)
    meta = [meta, lax.ppermute(meta, "exp", swap(2))]
    route = routing(first, meta, depth, *expert_ids.shape, local_experts, [weight_across[0]])

    behind = (z - jnp.arange(depth, dtype=jnp.int32)) % depth
    block = (behind[:, None] * 2 + jnp.stack([y, 1 - y])[None, :]).astype(jnp.int32)
    key_pos = (block.reshape(-1, 1) * rows + jnp.arange(rows, dtype=jnp.int32)).reshape(1, -1)
    context = attend(core, block[:, 0] * rows, key_pos, message, across, rows, columns)
    kept, given = project(
        block.reshape(-1), context, [part for d in range(depth) for part in (weight[d], weight_across[d])], route[1:]
    )
    chip = {d: wide(kept[d]) + wide(lax.ppermute(given[d], "exp", swap(2))) for d in steps + [0]}
    parts = [wide(stream) + chip[0]]
    for d in steps:
        parts.append(lax.ppermute(narrow(chip[d]), "seq", ring(size, -d)))
    return *add_up(parts), route


def routing(first, meta, subs, rows, top, local_experts, before):
    lines = rows // 4
    tokens = 4 * rows
    slots = 4 * CAP
    lanes = 128
    contract = lambda a, b, i, j: lax.dot_general(a, b, (((i,), (j,)), ((), ())), preferred_element_type=jnp.float32)
    iota = lambda shape, axis: lax.broadcasted_iota(jnp.int32, shape, axis)

    def kernel(first_ref, mine_ref, other_ref, *refs):
        select_ref, spread_ref, gate_ref = refs[len(before) :]
        token, other = iota((tokens, tokens), 0), iota((tokens, tokens), 1)
        earlier = narrow(wide((other < token) & (other // rows == token // rows)))
        same = narrow(wide(token == other))
        lane = iota((tokens, lanes), 1)
        owner = narrow(wide(iota((lanes, local_experts * slots), 1) // slots == iota((lanes, local_experts * slots), 0)))
        slot = iota((local_experts * slots, tokens), 0)
        fits = slot % slots // CAP == iota((local_experts * slots, tokens), 1) // rows
        for s in range(subs):
            packed = []
            for ref in (mine_ref, other_ref):
                for y in range(2):
                    block = wide(ref[(2 * s + y) * lines : (2 * s + y + 1) * lines, :])
                    packed += [block[:, g * HD // 2 : g * HD // 2 + 3 * top] for g in range(4)]
            packed = jnp.concatenate(packed, axis=0)
            hit = jnp.zeros((tokens, lanes), jnp.float32)
            high, low = hit, hit
            for j in range(local_experts):
                match = packed[:, :top] == wide(first_ref[0] + j)
                column = lambda kind: jnp.sum(jnp.where(match, kind, 0.0), axis=1, keepdims=True)
                here = lane == j
                hit = jnp.where(here, column(1.0), hit)
                high = jnp.where(here, column(packed[:, top : 2 * top]), high)
                low = jnp.where(here, column(packed[:, 2 * top :]), low)
            place = contract(earlier, narrow(hit), 1, 0)
            by_slot = lambda value: contract(owner, narrow(value), 0, 1)
            chosen = (by_slot(hit) > 0.5) & (jnp.abs(by_slot(place) - wide(slot % CAP)) < 0.5) & fits
            gates = jnp.sum(jnp.where(chosen, by_slot(high) + by_slot(low), 0.0), axis=1, keepdims=True)
            chosen = narrow(wide(chosen))
            spread_ref[s] = narrow(contract(same, chosen, 1, 1))
            for j in range(local_experts):
                select_ref[j, s] = chosen[j * slots : (j + 1) * slots]
                gate_ref[j, s * slots : (s + 1) * slots, :] = gates[j * slots : (j + 1) * slots]

    return pl.pallas_call(
        kernel,
        out_shape=[
            jax.ShapeDtypeStruct((local_experts, subs, slots, tokens), jnp.bfloat16),
            jax.ShapeDtypeStruct((subs, tokens, local_experts * slots), jnp.bfloat16),
            jax.ShapeDtypeStruct((local_experts, subs * slots, 1), jnp.float32),
        ],
        in_specs=[smem, vmem, vmem] + [unread] * len(before),
        out_specs=[vmem] * 3,
        compiler_params=limit(32),
        name="routing",
    )(first.astype(jnp.int32).reshape(1), *meta, *before)


def run_experts(mine, other, select, spread, row_gate, norm_gain, expert_in, expert_out):
    subs = len(mine)
    tokens, width = mine[0].shape
    local_experts, hidden, _ = expert_out.shape
    slots = select.shape[2]
    held = min(local_experts, 2)
    batch = min(subs, 4)
    room = 8 * subs * tokens * width + 6 * held * hidden * width + 4 * local_experts * subs * slots * width

    def kernel(select_ref, spread_ref, gate_ref, gain_ref, wi_ref, wo_ref, *refs):
        mine_refs, other_refs = refs[:subs], refs[subs : 2 * subs]
        kept_refs, given_refs = refs[2 * subs : 3 * subs], refs[3 * subs : 4 * subs]
        first, second, x, xg, res, sem = refs[4 * subs :]

        def copy(e, part):
            if part < 2:
                source, target = wi_ref.at[e, :, part * hidden : (part + 1) * hidden], first.at[e % held, part]
            else:
                source, target = wo_ref.at[e], second.at[e % held]
            return pltpu.make_async_copy(source, target, sem.at[e % held, part])

        def arrive(e, part):
            copy(e, part).wait()
            coming = 3 * e + part + AHEAD
            if coming < 3 * local_experts:
                copy(coming // 3, coming % 3).start()

        for part in range(AHEAD):
            copy(0, part).start()
        for s in range(subs):
            choose = select_ref[:, s].reshape(local_experts * slots, 2 * tokens)
            x[s % 2, :tokens, :] = mine_refs[s][...]
            x[s % 2, tokens:, :] = other_refs[s][...]
            picked = jnp.dot(choose, x[s % 2], preferred_element_type=jnp.float32)
            scale = lax.rsqrt(jnp.sum(picked * picked, axis=1, keepdims=True) * (1.0 / width) + 1e-06)
            rows = narrow(picked * scale * gain_ref[...])
            for e in range(local_experts):
                xg[e, s * slots : (s + 1) * slots, :] = rows[e * slots : (e + 1) * slots]
        for e in range(local_experts):
            for at in range(0, subs, batch):
                span = slice(at * slots, (at + batch) * slots)
                rows = xg[e, span, :]
                if at == 0:
                    arrive(e, 0)
                gate = jnp.dot(rows, first[e % held, 0], preferred_element_type=jnp.float32)
                if at == 0:
                    arrive(e, 1)
                up = jnp.dot(rows, first[e % held, 1], preferred_element_type=jnp.float32)
                act = narrow(gate / (1.0 + jnp.exp(-gate)) * up)
                if at == 0:
                    arrive(e, 2)
                part = jnp.dot(act, second[e % held], preferred_element_type=jnp.float32)
                scaled = narrow(part * gate_ref[e, span, :])
                for s in range(batch):
                    res[at + s, e * slots : (e + 1) * slots, :] = scaled[s * slots : (s + 1) * slots]
        for s in range(subs):
            both = narrow(jnp.dot(spread_ref[s], res[s], preferred_element_type=jnp.float32))
            kept_refs[s][...] = both[:tokens]
            given_refs[s][...] = both[tokens:]

    flops = local_experts * subs * slots * width * hidden * 6
    moved = (expert_in.size + expert_out.size + 8 * subs * tokens * width) * 2
    outs = pl.pallas_call(
        kernel,
        out_shape=[jax.ShapeDtypeStruct((tokens, width), jnp.bfloat16)] * (2 * subs),
        in_specs=[vmem] * 4 + [unread] * 2 + [vmem] * (2 * subs),
        out_specs=[vmem] * (2 * subs),
        scratch_shapes=[
            pltpu.VMEM((held, 2, width, hidden), jnp.bfloat16),
            pltpu.VMEM((held, hidden, width), jnp.bfloat16),
            pltpu.VMEM((2, 2 * tokens, width), jnp.bfloat16),
            pltpu.VMEM((local_experts, subs * slots, width), jnp.bfloat16),
            pltpu.VMEM((subs, local_experts * slots, width), jnp.bfloat16),
            pltpu.SemaphoreType.DMA((held, 3)),
        ],
        compiler_params=limit(room * 19 // 16 // 2**20),
        cost_estimate=pl.CostEstimate(flops=flops, bytes_accessed=moved, transcendentals=0),
        name="experts",
    )(select, spread, row_gate, norm_gain.reshape(1, -1), expert_in, expert_out, *mine, *other)
    return outs[:subs], outs[subs:]


def expert_block(mixed, rounded, route, norm_gain, expert_in, expert_out):
    size = lax.axis_size("seq")
    depth = size // 2
    rows = mixed.shape[0]

    along, mine, other = [rounded], [], []
    for d in range(depth):
        if d + 1 < depth:
            along.append(lax.ppermute(along[d], "seq", ring(size, 1)))
        if 0 < d == depth - 1:
            across = lax.ppermute(first, "seq", ring(size, d))
        else:
            across = lax.ppermute(along[d], "seq", swap(size))
        if d == 0:
            first = across
        mine.append(jnp.concatenate([along[d], across]))
        other.append(lax.ppermute(mine[d], "exp", swap(2)))
    kept, given = run_experts(mine, other, *route, norm_gain, expert_in, expert_out)

    pair = [wide(kept[d]) + wide(lax.ppermute(given[d], "exp", swap(2))) for d in range(depth)]
    last = depth - 1
    there = wide(lax.ppermute(narrow(pair[last]), "seq", ring(size, -last)))
    total = mixed + pair[0][:rows] + there[:rows]
    for d in far_first(depth):
        if d != last:
            chip = pair[d][:rows] + wide(lax.ppermute(narrow(pair[d][rows:]), "seq", swap(size)))
            total = total + wide(lax.ppermute(narrow(chip), "seq", ring(size, -d)))
    across = narrow(pair[0][rows:] + there[rows:])
    return narrow(total + wide(lax.ppermute(across, "seq", swap(size))))


def on_device(
    stream,
    queries,
    key_rows,
    value_rows,
    out_weight,
    norm_gain,
    expert_ids,
    gate_weights,
    expert_in,
    expert_out,
):
    mixed, rounded, route = attention_block(
        stream, queries, key_rows, value_rows, out_weight, expert_ids, gate_weights, expert_in.shape[0]
    )
    return expert_block(mixed, rounded, route, norm_gain, expert_in, expert_out)


def solution(mesh):
    in_specs = (
        P(("groups", "seq", "exp"), None),
        P(("groups", "seq"), "exp"),
        P(("groups", "seq"), "exp"),
        P(("groups", "seq"), "exp"),
        P("seq", "exp"),
        P(),
        P(("groups", "seq", "exp"), None),
        P(("groups", "seq", "exp"), None),
        P(("seq", "exp"), None, None),
        P(("seq", "exp"), None, None),
    )
    out_specs = P(("groups", "seq", "exp"), None)
    return jax.shard_map(
        on_device, mesh=mesh, in_specs=in_specs, out_specs=out_specs, check_vma=False
    )
```

```python
import jax
import jax.numpy as jnp
from jax import lax
from jax.experimental import pallas as pl
from jax.experimental.pallas import tpu as pltpu
from jax.sharding import PartitionSpec as P

HD = 128
CAP = 12
AHEAD = 3

neg_large = -1e30
smem = pl.BlockSpec(memory_space=pltpu.SMEM)
vmem = pl.BlockSpec(memory_space=pltpu.VMEM)
unread = pl.BlockSpec(memory_space=pl.ANY)


def limit(mebibytes):
    return pltpu.CompilerParams(vmem_limit_bytes=mebibytes * 1024 * 1024)


def ring(size, step):
    return [(i, (i + 2 * step) % size) for i in range(size)]


def swap(size):
    return [(i, i ^ 1) for i in range(size)]


def far_first(depth):
    return sorted(range(1, depth), key=lambda d: -min(d, depth - d))


def wide(value):
    return value.astype(jnp.float32)


def narrow(value):
    return value.astype(jnp.bfloat16)


def pack_heads(z, queries, key_rows, value_rows, expert_ids, gate_weights, depth):
    rows = queries.shape[0]
    columns = queries.shape[1] // depth
    per_group = queries.shape[1] // key_rows.shape[1] * HD
    top, tokens = expert_ids.shape
    lines = tokens // 4

    def kernel(z_ref, query_ref, key_ref, value_ref, id_ref, gate_ref, *out_refs):
        gates = gate_ref[...]
        high = wide(narrow(gates))
        blank = jnp.zeros((HD // 2 - 3 * top, tokens), jnp.float32)
        meta = jnp.concatenate([wide(id_ref[...]), high, gates - high, blank], axis=0).T
        meta = jnp.concatenate([meta[g * lines : (g + 1) * lines] for g in range(4)], axis=1)
        for d, out_ref in enumerate(out_refs[:depth]):
            start = (z_ref[0] + d) % depth * columns
            group = pl.ds(pl.multiple_of(start // per_group * HD, HD), HD)
            out_ref[:rows, :columns] = query_ref[:, pl.ds(pl.multiple_of(start, HD), columns)]
            out_ref[:rows, columns : columns + HD] = key_ref[:, group]
            out_ref[:rows, columns + HD :] = value_ref[:, group]
            out_ref[rows:, :columns] = jnp.zeros((lines, columns), jnp.bfloat16)
            out_ref[rows:, columns:] = narrow(meta)
        out_refs[depth][...] = out_refs[0][:, columns:]

    return pl.pallas_call(
        kernel,
        out_shape=[jax.ShapeDtypeStruct((rows + lines, columns + 2 * HD), queries.dtype)] * depth
        + [jax.ShapeDtypeStruct((rows + lines, 2 * HD), queries.dtype)],
        in_specs=[smem] + [vmem] * 5,
        out_specs=[vmem] * (depth + 1),
        compiler_params=limit(56),
        name="pack_heads",
    )(z, queries, key_rows, value_rows, expert_ids, gate_weights)


def pack_weight(z, out_weight, depth, before):
    rows = out_weight.shape[0]
    columns = out_weight.shape[1] // depth

    def kernel(z_ref, weight_ref, *refs):
        for d, out_ref in enumerate(refs[len(before) :]):
            start = pl.multiple_of((z_ref[0] + d) % depth * columns, HD)
            out_ref[...] = weight_ref[:, pl.ds(start, columns)]

    return pl.pallas_call(
        kernel,
        out_shape=[jax.ShapeDtypeStruct((rows, columns), out_weight.dtype)] * depth,
        in_specs=[smem, vmem] + [unread] * len(before),
        out_specs=[vmem] * depth,
        compiler_params=limit(16),
        name="pack_weight",
    )(z, out_weight, *before)


def collect_meta(near, across, rows):
    lines = across[0].shape[0] - rows
    parts = [part for pair in zip(near, across) for part in pair]

    def kernel(*refs):
        for i, ref in enumerate(refs[:-1]):
            refs[-1][i * lines : (i + 1) * lines, :] = ref[rows:, -2 * HD :]

    return pl.pallas_call(
        kernel,
        out_shape=jax.ShapeDtypeStruct((len(parts) * lines, 2 * HD), jnp.bfloat16),
        in_specs=[vmem] * len(parts),
        out_specs=vmem,
        compiler_params=limit(16),
        name="collect_meta",
    )(*parts)


def attend(core, starts, key_pos, messages, across, rows, columns):
    depth = len(messages)
    heads = columns // HD
    length = 2 * depth * rows
    half = rows // 2

    def kernel(core_ref, starts_ref, key_pos_ref, *refs):
        message_refs, across_refs = refs[:depth], refs[depth : 2 * depth]
        out_refs, (query, keyed) = refs[-2 - depth : -2], refs[-2:]
        for d in range(depth):
            for h in range(heads):
                query[d, h * rows : (h + 1) * rows, :] = message_refs[d][:rows, h * HD : (h + 1) * HD]
            keyed[2 * d * rows : (2 * d + 1) * rows, :] = message_refs[d][:rows, columns:]
            keyed[(2 * d + 1) * rows : (2 * d + 2) * rows, :] = across_refs[d][:rows, :]
        mine = core_ref[0] == 0

        for d in range(depth):
            scores = lax.dot_general(
                query[d], keyed[:, :HD], (((1,), (1,)), ((), ())), preferred_element_type=jnp.float32
            )
            offset = lax.broadcasted_iota(jnp.int32, (heads * rows, 1), 0) % rows
            allowed = key_pos_ref[...] <= starts_ref[d] + offset
            scores = jnp.where(allowed, scores, neg_large)
            largest = jnp.max(scores, axis=-1, keepdims=True)
            exps = jnp.exp((scores - largest) * (HD**-0.5))
            total = jnp.sum(exps, axis=-1, keepdims=True)
            summed = jnp.dot(narrow(exps), keyed[:, HD:], preferred_element_type=jnp.float32)
            context = narrow(summed / total)
            for h in range(heads):
                low, high = context[h * rows : h * rows + half], context[h * rows + half : (h + 1) * rows]
                out_refs[d][:half, h * HD : (h + 1) * HD] = jnp.where(mine, low, high)
                out_refs[d][half:, h * HD : (h + 1) * HD] = jnp.where(mine, high, low)

    work = depth * rows * columns * length
    return pl.pallas_call(
        kernel,
        out_shape=[jax.ShapeDtypeStruct((rows, columns), jnp.bfloat16)] * depth,
        in_specs=[smem, smem, vmem] + [vmem] * (2 * depth),
        out_specs=[vmem] * depth,
        scratch_shapes=[
            pltpu.VMEM((depth, heads * rows, HD), jnp.bfloat16),
            pltpu.VMEM((length, 2 * HD), jnp.bfloat16),
        ],
        compiler_params=limit(24),
        cost_estimate=pl.CostEstimate(flops=4 * work, bytes_accessed=depth * rows * columns * 8, transcendentals=work // HD),
        name="attend",
    )(core, starts, key_pos, *messages, *across)


def project(place, context, weights, before):
    depth, blocks = len(context), len(weights)
    rows, columns = context[0].shape[0] // 2, context[0].shape[1]
    features = weights[0].shape[0]
    shape = (rows, blocks * features)
    if features % HD:
        weight = jnp.stack(weights)[jnp.argsort(place)]
        left = jnp.stack(context).reshape(depth, 2, rows, columns)
        result = jnp.einsum("dcrk,bfk->cdrbf", left, weight, preferred_element_type=jnp.float32)
        result = narrow(result.reshape((2, depth) + shape))
        return [[result[core, d] for d in range(depth)] for core in range(2)]

    def kernel(place_ref, *refs):
        context_refs, weight_refs, out_refs = refs[:depth], refs[depth : depth + blocks], refs[-1 - 2 * depth : -1]
        left_ref = refs[-1]
        for d in range(depth):
            left_ref[2 * d * rows : 2 * (d + 1) * rows, :] = context_refs[d][...]
        left = left_ref[...]
        for i in range(blocks):
            part = narrow(
                lax.dot_general(
                    left, weight_refs[i][...], (((1,), (1,)), ((), ())), preferred_element_type=jnp.float32
                )
            ).reshape(depth, 2, rows, features)
            there = pl.ds(pl.multiple_of(place_ref[i] * features, HD), features)
            for d in range(depth):
                for core in range(2):
                    out_refs[core * depth + d][:, there] = part[d, core]

    outs = pl.pallas_call(
        kernel,
        out_shape=[jax.ShapeDtypeStruct(shape, jnp.bfloat16)] * (2 * depth),
        in_specs=[smem] + [vmem] * (depth + blocks) + [unread] * len(before),
        out_specs=[vmem] * (2 * depth),
        scratch_shapes=[pltpu.VMEM((2 * depth * rows, columns), jnp.bfloat16)],
        compiler_params=limit(20),
        cost_estimate=pl.CostEstimate(
            flops=4 * depth * rows * columns * blocks * features,
            bytes_accessed=2 * blocks * features * columns + 4 * depth * rows * (columns + 2 * blocks * features),
            transcendentals=0,
        ),
        name="project",
    )(place, *context, *weights, *before)
    return outs[:depth], outs[depth:]


def add_up(parts):
    def kernel(*refs):
        total = wide(refs[0][...])
        for ref in refs[1 : len(parts)]:
            total = total + wide(ref[...])
        refs[-2][...] = total
        refs[-1][...] = narrow(total)

    return pl.pallas_call(
        kernel,
        out_shape=[
            jax.ShapeDtypeStruct(parts[0].shape, jnp.float32),
            jax.ShapeDtypeStruct(parts[0].shape, jnp.bfloat16),
        ],
        in_specs=[vmem] * len(parts),
        out_specs=[vmem, vmem],
        compiler_params=limit(32),
        name="add_up",
    )(*parts)


def attention_block(stream, queries, key_rows, value_rows, out_weight, expert_ids, gate_weights, local_experts):
    size = lax.axis_size("seq")
    depth = size // 2
    z, y = lax.axis_index("seq") // 2, lax.axis_index("seq") % 2
    core = lax.axis_index("exp").astype(jnp.int32).reshape(1)
    rows = queries.shape[0]
    columns = queries.shape[1] // depth
    steps = far_first(depth)
    here = z.astype(jnp.int32).reshape(1)

    *message, keyed = pack_heads(here, queries, key_rows, value_rows, expert_ids.T, gate_weights.T, depth)
    for d in steps:
        message[d] = lax.ppermute(message[d], "seq", ring(size, d))
    across = {}
    for d in [0] + steps:
        across[d] = lax.ppermute(message[d][:, columns:] if d else keyed, "seq", swap(size))
    across = [across[d] for d in range(depth)]
    weight = list(pack_weight(here, out_weight, depth, [message[steps[0]]]))
    weight_across = {0: lax.ppermute(weight[0], "seq", swap(size))}
    for d in steps[::-1]:
        weight[d] = lax.ppermute(weight[d], "seq", ring(size, d))
        weight_across[d] = lax.ppermute(weight[d], "seq", swap(size))
    first = (lax.axis_index("seq") * 2 + lax.axis_index("exp")) * local_experts
    meta = collect_meta(message, across, rows)
    meta = [meta, lax.ppermute(meta, "exp", swap(2))]
    route = routing(first, meta, depth, *expert_ids.shape, local_experts, [weight_across[0]])

    behind = (z - jnp.arange(depth, dtype=jnp.int32)) % depth
    block = (behind[:, None] * 2 + jnp.stack([y, 1 - y])[None, :]).astype(jnp.int32)
    key_pos = (block.reshape(-1, 1) * rows + jnp.arange(rows, dtype=jnp.int32)).reshape(1, -1)
    context = attend(core, block[:, 0] * rows, key_pos, message, across, rows, columns)
    kept, given = project(
        block.reshape(-1), context, [part for d in range(depth) for part in (weight[d], weight_across[d])], route[1:]
    )
    chip = {d: wide(kept[d]) + wide(lax.ppermute(given[d], "exp", swap(2))) for d in steps + [0]}
    parts = [wide(stream) + chip[0]]
    for d in steps:
        parts.append(lax.ppermute(narrow(chip[d]), "seq", ring(size, -d)))
    return *add_up(parts), route


def routing(first, meta, subs, rows, top, local_experts, before):
    lines = rows // 4
    tokens = 4 * rows
    slots = 4 * CAP
    lanes = 128
    contract = lambda a, b, i, j: lax.dot_general(a, b, (((i,), (j,)), ((), ())), preferred_element_type=jnp.float32)
    iota = lambda shape, axis: lax.broadcasted_iota(jnp.int32, shape, axis)

    def kernel(first_ref, mine_ref, other_ref, *refs):
        select_ref, spread_ref, gate_ref = refs[len(before) :]
        token, other = iota((tokens, tokens), 0), iota((tokens, tokens), 1)
        earlier = narrow(wide((other < token) & (other // rows == token // rows)))
        same = narrow(wide(token == other))
        lane = iota((tokens, lanes), 1)
        owner = narrow(wide(iota((lanes, local_experts * slots), 1) // slots == iota((lanes, local_experts * slots), 0)))
        slot = iota((local_experts * slots, tokens), 0)
        fits = slot % slots // CAP == iota((local_experts * slots, tokens), 1) // rows
        for s in range(subs):
            packed = []
            for ref in (mine_ref, other_ref):
                for y in range(2):
                    block = wide(ref[(2 * s + y) * lines : (2 * s + y + 1) * lines, :])
                    packed += [block[:, g * HD // 2 : g * HD // 2 + 3 * top] for g in range(4)]
            packed = jnp.concatenate(packed, axis=0)
            hit = jnp.zeros((tokens, lanes), jnp.float32)
            high, low = hit, hit
            for j in range(local_experts):
                match = packed[:, :top] == wide(first_ref[0] + j)
                column = lambda kind: jnp.sum(jnp.where(match, kind, 0.0), axis=1, keepdims=True)
                here = lane == j
                hit = jnp.where(here, column(1.0), hit)
                high = jnp.where(here, column(packed[:, top : 2 * top]), high)
                low = jnp.where(here, column(packed[:, 2 * top :]), low)
            place = contract(earlier, narrow(hit), 1, 0)
            by_slot = lambda value: contract(owner, narrow(value), 0, 1)
            chosen = (by_slot(hit) > 0.5) & (jnp.abs(by_slot(place) - wide(slot % CAP)) < 0.5) & fits
            gates = jnp.sum(jnp.where(chosen, by_slot(high) + by_slot(low), 0.0), axis=1, keepdims=True)
            chosen = narrow(wide(chosen))
            spread_ref[s] = narrow(contract(same, chosen, 1, 1))
            for j in range(local_experts):
                select_ref[j, s] = chosen[j * slots : (j + 1) * slots]
                gate_ref[j, s * slots : (s + 1) * slots, :] = gates[j * slots : (j + 1) * slots]

    return pl.pallas_call(
        kernel,
        out_shape=[
            jax.ShapeDtypeStruct((local_experts, subs, slots, tokens), jnp.bfloat16),
            jax.ShapeDtypeStruct((subs, tokens, local_experts * slots), jnp.bfloat16),
            jax.ShapeDtypeStruct((local_experts, subs * slots, 1), jnp.float32),
        ],
        in_specs=[smem, vmem, vmem] + [unread] * len(before),
        out_specs=[vmem] * 3,
        compiler_params=limit(32),
        name="routing",
    )(first.astype(jnp.int32).reshape(1), *meta, *before)


def run_experts(pieces, select, spread, row_gate, norm_gain, expert_in, expert_out):
    subs = len(pieces)
    counts = [len(arrays) for arrays in pieces]
    flat = [array for arrays in pieces for array in arrays]
    tokens, width = sum(array.shape[0] for array in pieces[0]) // 2, flat[0].shape[1]
    local_experts, hidden, _ = expert_out.shape
    slots = select.shape[2]
    held = min(local_experts, 2)
    batch = min(subs, 4)
    room = 8 * subs * tokens * width + 6 * held * hidden * width + 4 * local_experts * subs * slots * width

    def kernel(select_ref, spread_ref, gate_ref, gain_ref, wi_ref, wo_ref, *refs):
        piece_refs, refs = refs[: len(flat)], refs[len(flat) :]
        kept_refs, given_refs = refs[:subs], refs[subs : 2 * subs]
        first, second, x, xg, res, sem = refs[2 * subs :]

        def copy(e, part):
            if part < 2:
                source, target = wi_ref.at[e, :, part * hidden : (part + 1) * hidden], first.at[e % held, part]
            else:
                source, target = wo_ref.at[e], second.at[e % held]
            return pltpu.make_async_copy(source, target, sem.at[e % held, part])

        def arrive(e, part):
            copy(e, part).wait()
            coming = 3 * e + part + AHEAD
            if coming < 3 * local_experts:
                copy(coming // 3, coming % 3).start()

        for part in range(AHEAD):
            copy(0, part).start()
        for s in range(subs):
            choose = select_ref[:, s].reshape(local_experts * slots, 2 * tokens)
            at = 0
            for ref in piece_refs[sum(counts[:s]) : sum(counts[: s + 1])]:
                x[s % 2, at : at + ref.shape[0], :] = ref[...]
                at += ref.shape[0]
            picked = jnp.dot(choose, x[s % 2], preferred_element_type=jnp.float32)
            scale = lax.rsqrt(jnp.sum(picked * picked, axis=1, keepdims=True) * (1.0 / width) + 1e-06)
            rows = narrow(picked * scale * gain_ref[...])
            for e in range(local_experts):
                xg[e, s * slots : (s + 1) * slots, :] = rows[e * slots : (e + 1) * slots]
        for e in range(local_experts):
            for at in range(0, subs, batch):
                span = slice(at * slots, (at + batch) * slots)
                rows = xg[e, span, :]
                if at == 0:
                    arrive(e, 0)
                gate = jnp.dot(rows, first[e % held, 0], preferred_element_type=jnp.float32)
                if at == 0:
                    arrive(e, 1)
                up = jnp.dot(rows, first[e % held, 1], preferred_element_type=jnp.float32)
                act = narrow(gate / (1.0 + jnp.exp(-gate)) * up)
                if at == 0:
                    arrive(e, 2)
                part = jnp.dot(act, second[e % held], preferred_element_type=jnp.float32)
                scaled = narrow(part * gate_ref[e, span, :])
                for s in range(batch):
                    res[at + s, e * slots : (e + 1) * slots, :] = scaled[s * slots : (s + 1) * slots]
        for s in range(subs):
            both = narrow(jnp.dot(spread_ref[s], res[s], preferred_element_type=jnp.float32))
            kept_refs[s][...] = both[:tokens]
            given_refs[s][...] = both[tokens:]

    flops = local_experts * subs * slots * width * hidden * 6
    moved = (expert_in.size + expert_out.size + 8 * subs * tokens * width) * 2
    outs = pl.pallas_call(
        kernel,
        out_shape=[jax.ShapeDtypeStruct((tokens, width), jnp.bfloat16)] * (2 * subs),
        in_specs=[vmem] * 4 + [unread] * 2 + [vmem] * len(flat),
        out_specs=[vmem] * (2 * subs),
        scratch_shapes=[
            pltpu.VMEM((held, 2, width, hidden), jnp.bfloat16),
            pltpu.VMEM((held, hidden, width), jnp.bfloat16),
            pltpu.VMEM((2, 2 * tokens, width), jnp.bfloat16),
            pltpu.VMEM((local_experts, subs * slots, width), jnp.bfloat16),
            pltpu.VMEM((subs, local_experts * slots, width), jnp.bfloat16),
            pltpu.SemaphoreType.DMA((held, 3)),
        ],
        compiler_params=limit(room * 19 // 16 // 2**20),
        cost_estimate=pl.CostEstimate(flops=flops, bytes_accessed=moved, transcendentals=0),
        name="experts",
    )(select, spread, row_gate, norm_gain.reshape(1, -1), expert_in, expert_out, *flat)
    return outs[:subs], outs[subs:]


def expert_block(mixed, rounded, route, norm_gain, expert_in, expert_out):
    size = lax.axis_size("seq")
    depth = size // 2
    rows = mixed.shape[0]

    along, pieces = [rounded], []
    for d in range(depth):
        if d + 1 < depth:
            along.append(lax.ppermute(along[d], "seq", ring(size, 1)))
        if 0 < d == depth - 1:
            across = lax.ppermute(first, "seq", ring(size, d))
        else:
            across = lax.ppermute(along[d], "seq", swap(size))
        if d == 0:
            first = across
        mine = [along[d], across]
        if d + 1 < depth:
            mine = [jnp.concatenate(mine)]
        pieces.append(mine + [lax.ppermute(part, "exp", swap(2)) for part in mine])
    kept, given = run_experts(pieces, *route, norm_gain, expert_in, expert_out)

    pair = [wide(kept[d]) + wide(lax.ppermute(given[d], "exp", swap(2))) for d in range(depth)]
    last = depth - 1
    there = wide(lax.ppermute(narrow(pair[last]), "seq", ring(size, -last)))
    total = mixed + pair[0][:rows] + there[:rows]
    for d in far_first(depth):
        if d != last:
            chip = pair[d][:rows] + wide(lax.ppermute(narrow(pair[d][rows:]), "seq", swap(size)))
            total = total + wide(lax.ppermute(narrow(chip), "seq", ring(size, -d)))
    across = narrow(pair[0][rows:] + there[rows:])
    return narrow(total + wide(lax.ppermute(across, "seq", swap(size))))


def on_device(
    stream,
    queries,
    key_rows,
    value_rows,
    out_weight,
    norm_gain,
    expert_ids,
    gate_weights,
    expert_in,
    expert_out,
):
    mixed, rounded, route = attention_block(
        stream, queries, key_rows, value_rows, out_weight, expert_ids, gate_weights, expert_in.shape[0]
    )
    return expert_block(mixed, rounded, route, norm_gain, expert_in, expert_out)


def solution(mesh):
    in_specs = (
        P(("groups", "seq", "exp"), None),
        P(("groups", "seq"), "exp"),
        P(("groups", "seq"), "exp"),
        P(("groups", "seq"), "exp"),
        P("seq", "exp"),
        P(),
        P(("groups", "seq", "exp"), None),
        P(("groups", "seq", "exp"), None),
        P(("seq", "exp"), None, None),
        P(("seq", "exp"), None, None),
    )
    out_specs = P(("groups", "seq", "exp"), None)
    return jax.shard_map(
        on_device, mesh=mesh, in_specs=in_specs, out_specs=out_specs, check_vma=False
    )
```
